512 devices in a mesh: inst: 16 (over y, x_hi), tp: 32 (over z, x_lo, core).
Axes of the slice: x: 4 (x_hi: 2, x_lo: 2; x = x_hi * 2 + x_lo), y: 8, z: 8, core: 2. Of those that a mesh axis runs over, the one named last changes fastest.
Arguments:
- tokens: bfloat16 [2560, 8192], P('inst'), as said below
- doc_ids: int32 [16, 160], replicated, may hold values from 0 to 3, never falling along the last dimension, each value on 1 to 80 neighbouring positions
- query_one: bfloat16 [8192, 4096], P('inst', 'tp'), as said below
- keyval_one: bfloat16 [8192, 1024], P('inst', 'tp'), as said below
- output_one: bfloat16 [4096, 8192], P('tp', 'inst'), may hold values from -0.09375 to 0.09375
- query_two: bfloat16 [8192, 4096], P('inst', 'tp'), as said below
- keyval_two: bfloat16 [8192, 1024], P('inst', 'tp'), as said below
- output_two: bfloat16 [4096, 8192], P('tp', 'inst'), may hold values from -0.1875 to 0.1875
Outputs:
- blended: bfloat16 [2560, 8192], P('inst', 'tp')
The draws below stay inside these ranges and needn't reach their ends.
Inputs may be any that keep to these rules, and one draw needn't show every extreme that they name: `doc_ids`: along each row the document numbers never fall; each document holds 1 to 80 positions. `query_one`: A projection scaled by the square root of its fan-in. `keyval_one`: A projection scaled by the square root of its fan-in. `query_two`: A projection scaled by the square root of its fan-in. `keyval_two`: A projection scaled by the square root of its fan-in. `tokens`: hidden rows of order one.
All inputs are finite; a program needn't handle non-finite values.
Results may differ from the reference program's by a relative error of at most 0.034.
Values may be sent and summed in bfloat16 or wider, within the bound.
A program may use at most 64 MiB of HBM per device.

```python
import math
import jax
import jax.numpy as jnp
import numpy as np
from jax import lax

D = 8192
HD = 128
GROUP = 8
TOK_INST = 160
DOCS = 4
TOKENS = 2560
HQ = 32
KVH = 4
MOST = 80
N_INST = 16
N_TP = 32


def query_law(key):
    noise = jax.random.normal(key, (D, HQ, HD), jnp.float32) * D ** (-0.5)
    mixed = noise
    return mixed.reshape(D, HQ * HD).astype(jnp.bfloat16)


def keyval_law(key):
    noise = jax.random.normal(key, (D, KVH, 2, HD), jnp.float32) * D ** (-0.5)
    key_part = noise[:, :, 0]
    both = jnp.stack([key_part, noise[:, :, 1]], axis=2)
    return both.reshape(D, KVH * 2 * HD).astype(jnp.bfloat16)


def draw_tokens(key, part):
    key = jax.random.fold_in(key, 3)
    first, second, third = jax.random.split(key, 3)
    row_scale = jnp.exp(jax.random.uniform(first, (TOKENS, 1), jnp.float32, -1.15, 1.15))
    col_scale = jnp.exp(jax.random.uniform(second, (1, D), jnp.float32, -1.15, 1.15))
    base = jax.random.normal(third, (TOKENS, D), jnp.float32)
    return (0.5 * base * row_scale * col_scale).astype(jnp.bfloat16)


def draw_query_one(key, part):
    key = jax.random.fold_in(key, 21)
    return query_law(key)


def draw_keyval_one(key, part):
    key = jax.random.fold_in(key, 22)
    return keyval_law(key)


def draw_query_two(key, part):
    key = jax.random.fold_in(key, 23)
    return query_law(key)


def draw_keyval_two(key, part):
    key = jax.random.fold_in(key, 24)
    return keyval_law(key)


def raised(entries, key, source, target, shards_of, factor):
    owner, partner = [(jnp.arange(entries.shape[dim]) // (entries.shape[dim] // shards_of)).reshape([-1 if axis == dim else 1 for axis in range(entries.ndim)]) for dim in (source, target)]
    chosen = jax.random.permutation(key, shards_of)[partner]
    strong = (owner == chosen) | (owner == (partner + shards_of // 2) % shards_of)
    return jnp.where(strong, factor * entries, entries)


def shard_levels(stream_key, extent, cuts, least, largest):
    loudness = 1.0
    for dim, shards_of in cuts:
        draws = jax.random.uniform(jax.random.fold_in(jax.random.fold_in(stream_key, 6), dim), (shards_of,), jnp.float32, least / len(cuts), largest / len(cuts))
        loudness = loudness * jnp.repeat(jnp.exp(draws), extent[dim] // shards_of).reshape((-1,) + (1,) * (len(extent) - 1 - dim))
    return loudness


def split_up(amount, total, bound, slope):
    weights = [(1 << 20) // math.isqrt(standing ** slope) + 1 for standing in range(2, amount + 1)]
    surplus, counts = total - bound - (amount - 1), [1] * (amount - 1)
    while surplus > 0:
        movable = [i for i in range(amount - 1) if counts[i] < bound]
        whole, budget = sum([weights[i] for i in movable]), surplus
        for i in movable:
            more = min(bound - counts[i], max(1, budget * weights[i] // whole), surplus)
            counts[i] = counts[i] + more
            surplus = surplus - more
    return np.array([bound] + counts)


def ragged(own_key, amount, total, reach, skew):
    if amount == 2:
        one = jax.random.randint(own_key, (), max(1, total - reach), min(reach, total - 1) + 1)
        return jnp.stack([one, total - one])
    lengths = jnp.asarray(split_up(amount, total, reach, skew), jnp.int32)
    couples = (amount - 1) // 2
    donor, sink = lengths[1:1 + 2 * couples:2], lengths[2:2 + 2 * couples:2]
    room = jnp.minimum(donor - 1, reach - sink)
    moved = jax.random.randint(jax.random.fold_in(own_key, 1), (couples,), 0, 1 << 20) % (room + 1)
    lengths = lengths.at[1:1 + 2 * couples:2].set(donor - moved).at[2:2 + 2 * couples:2].set(sink + moved)
    return lengths[jax.random.permutation(jax.random.fold_in(own_key, 2), amount)]


def normal_values(key, dims, width, reach, cuts=(), kind=jnp.bfloat16):
    level = shard_levels(key, dims, cuts, -0.22, 0.18) if cuts else 1.0
    values = jax.random.normal(key, dims, jnp.float32) * width * level
    return jnp.minimum(jnp.maximum(values, -reach), reach).astype(kind)


def heavy_noise(own_key, extent, spread, limit, pieces, heavy, kind=jnp.bfloat16):
    values = spread * jax.random.normal(own_key, extent, jnp.float32)
    if pieces:
        values = values * shard_levels(own_key, extent, pieces, -0.22, 0.18)
    return jnp.clip(raised(values, jax.random.fold_in(own_key, 3), *heavy), -limit, limit).astype(kind)


def setup_inputs(seed: int = 0) -> dict:
    keys = jax.random.split(jax.random.key(seed), 9)
    return {
        "tokens": draw_tokens(jax.random.fold_in(keys[8], 71), 0),
        "doc_ids": jax.vmap(lambda own: jnp.searchsorted(jnp.cumsum(ragged(own, DOCS, TOK_INST, MOST, 2)), jnp.arange(TOK_INST), side="right"))(jax.random.split(keys[1], N_INST)).reshape((N_INST, TOK_INST)).astype(jnp.int32),
        "query_one": draw_query_one(jax.random.fold_in(keys[8], 71), 0),
        "keyval_one": draw_keyval_one(jax.random.fold_in(keys[8], 71), 0),
        "output_one": normal_values(keys[4], (HQ * HD, D), (HQ * HD) ** -0.5, 0.09375, ((0, 32), (1, 16))),
        "query_two": draw_query_two(jax.random.fold_in(keys[8], 71), 0),
        "keyval_two": draw_keyval_two(jax.random.fold_in(keys[8], 71), 0),
        "output_two": heavy_noise(keys[7], (HQ * HD, D), (HQ * HD) ** -0.5, 0.1875, ((0, 32), (1, 16)), (0, 1, 32, 2.75)),
    }


def normalize(hidden):
    floats = hidden.astype(jnp.float32)
    scale = lax.rsqrt(lax.optimization_barrier(jnp.mean(floats * floats, axis=1, keepdims=True)) + 1e-06)
    return (floats * scale).astype(jnp.bfloat16)

def attend(hidden, docs, query_weight, keyval_weight, output_weight):
    normed = normalize(hidden)
    queries = (jnp.dot(normed, query_weight, preferred_element_type=jnp.float32) * HD ** (-0.5)).astype(jnp.bfloat16)
    keyvals = jnp.dot(normed, keyval_weight, preferred_element_type=jnp.float32).astype(jnp.bfloat16)
    query_rows = queries.reshape(N_INST, TOK_INST, HQ, HD).astype(jnp.float32)
    split_kv = keyvals.reshape(N_INST, TOK_INST, KVH, 2, HD).astype(jnp.float32)
    key_rows = jnp.repeat(split_kv[:, :, :, 0], GROUP, axis=2)
    value_rows = jnp.repeat(split_kv[:, :, :, 1], GROUP, axis=2)
    scores = jnp.einsum('ntha,nsha->nhts', query_rows, key_rows, precision=lax.Precision.HIGHEST)
    position = jnp.arange(TOK_INST)
    allowed = (docs[:, :, None] == docs[:, None, :]) & (position[None, None, :] <= position[None, :, None])
    scores = jnp.where(allowed[:, None], scores, -1e+30)
    row_top = lax.optimization_barrier(jnp.max(scores, axis=3, keepdims=True))
    weights = jnp.exp(scores - row_top)
    probabilities = (weights / lax.optimization_barrier(jnp.sum(weights, axis=3, keepdims=True))).astype(jnp.bfloat16)
    context = jnp.einsum('nhts,nsha->ntha', probabilities.astype(jnp.float32), value_rows, precision=lax.Precision.HIGHEST)
    context = context.astype(jnp.bfloat16).reshape(TOKENS, HQ * HD)
    per_rank = HQ * HD // N_TP
    context_groups = context.reshape(TOKENS, N_TP, per_rank).transpose(1, 0, 2)
    output_groups = output_weight.reshape(N_TP, per_rank, D)

    def add_group(total, pair):
        term = jnp.dot(pair[0], pair[1], preferred_element_type=jnp.float32)
        rounded = lax.optimization_barrier(term.astype(jnp.bfloat16))
        return (total + rounded.astype(jnp.float32), None)
    total, unused = lax.scan(add_group, jnp.zeros((TOKENS, D), jnp.float32), (context_groups, output_groups))
    return total

def reference(tokens, doc_ids, query_one, keyval_one, output_one, query_two, keyval_two, output_two):
    attended_one = attend(tokens, doc_ids, query_one, keyval_one, output_one)
    middle = (tokens.astype(jnp.float32) + attended_one).astype(jnp.bfloat16)
    arrived = jnp.roll(middle, TOK_INST, axis=0)
    arrived_docs = jnp.roll(doc_ids, 1, axis=0)
    attended_two = attend(arrived, arrived_docs, query_two, keyval_two, output_two)
    return (arrived.astype(jnp.float32) + attended_two).astype(jnp.bfloat16)
```

```python
import functools

import jax
import jax.numpy as jnp
from jax import lax
from jax.experimental import pallas as pl
from jax.experimental.pallas import tpu as pltpu
from jax.sharding import PartitionSpec as P

MESH = pl.DeviceIdType.MESH
F32 = jnp.float32
BF16 = jnp.bfloat16
NT = (((1,), (1,)), ((), ()))
ROWS = 160
HEAD = 128
PIECE = 32
WIDE = 256
GROUP = 8
REACH = ((4, 3), (3, 4))


def dot_nt(left, right):
    return lax.dot_general(left, right, NT, preferred_element_type=F32)


def kernel(
    ny,
    nz,
    tokens,
    docs,
    query_one,
    keyval_one,
    output_one,
    query_two,
    keyval_two,
    output_two,
    out,
    wq,
    wkv,
    wo,
    kvin,
    kvt,
    docs_in,
    mask,
    xs,
    aq,
    akv,
    ass,
    near_s,
    near_r,
    far_s,
    far_r,
    tail_pad,
    kvs,
    ctx,
    pbuf,
    rs_s,
    rs_r,
    half_s,
    half_r,
    fin,
    local_sem,
    xlocal_sem,
    swap_ss,
    swap_rs,
    y_ss,
    y_rs,
    tok_ss,
    tok_rs,
    near_ss,
    near_rs,
    far_ss,
    far_rs,
    kv_ss,
    kv_rs,
    ctx_ss,
    ctx_rs,
    z_ss,
    z_rs,
    half_ss,
    half_rs,
    ag_ss,
    ag_rs,
    one_ss,
    one_rs,
):
    inst = lax.axis_index("inst")
    rank = lax.axis_index("tp")
    ninst, nrank = 2 * ny, 4 * nz
    y, x_hi = inst // 2, inst % 2
    z, x_lo, c = rank // 4, rank // 2 % 2, rank % 2
    piece = rank % GROUP
    model = ny * 2 * 512

    mate = (inst, rank + 1 - 2 * c)
    across = (inst + 1 - 2 * x_hi, rank)
    across_mate = (inst + 1 - 2 * x_hi, rank + 1 - 2 * c)
    beside = (inst, rank + 2 - 4 * x_lo)
    y_next = (((inst + 2) % ninst, rank), ((inst + ninst - 2) % ninst, rank))
    z_next = ((inst, (rank + 4) % nrank), (inst, (rank + nrank - 4) % nrank))
    goal = ((2 * y + x_lo + 1) % ninst, 4 * z + 2 * x_hi + c)
    origin_inst = (inst + ninst - 1) % ninst
    origin = (origin_inst // 2 * 2 + rank // 2 % 2, 4 * z + 2 * (1 - x_hi) + c)

    group_base = rank // GROUP * GROUP
    sharers = [(inst, group_base + (piece + o) % GROUP) for o in range(1, GROUP)]
    other_z = (inst, (rank + nrank + 4 * (2 * (z % 2) - 1)) % nrank)

    barrier = pltpu.get_barrier_semaphore()
    greeted = sharers + [other_z, y_next[0], y_next[1], across, across_mate, origin]
    for peer in greeted:
        pl.semaphore_signal(barrier, inc=1, device_id=peer, device_id_type=MESH)

    sent = []

    def copy(src, dst, send, recv, peer):
        return pltpu.make_async_remote_copy(
            src_ref=src,
            dst_ref=dst,
            send_sem=send,
            recv_sem=recv,
            device_id=peer,
            device_id_type=MESH,
        )

    def send(*args):
        move = copy(*args)
        move.start()
        sent.append(move)

    def landed(dst, send_sem, recv_sem):
        copy(dst, dst, send_sem, recv_sem, mate).wait_recv()

    queries = (query_one, query_two)
    keyvals = (keyval_one, keyval_two)
    outputs = (output_one, output_two)
    loads = {}

    def load(name, src, dst, sem):
        loads[name] = pltpu.make_async_copy(src, dst, sem)
        loads[name].start()

    def quarter(block, hi):
        return pl.ds(pl.multiple_of((2 * block + hi) * 512 + c * WIDE, WIDE), WIDE)

    own_k = pl.ds(pl.multiple_of(c * WIDE, WIDE), WIDE)
    mate_k = pl.ds(pl.multiple_of((1 - c) * WIDE, WIDE), WIDE)
    load("kv0", keyvals[0], kvin.at[0], local_sem.at[0])
    load("q0", queries[0].at[own_k, :], wq.at[0, y, c], local_sem.at[1])
    for b in range(nz):
        load(("x", b), tokens.at[:, quarter(b, x_hi)], xs.at[0, b, x_hi], xlocal_sem.at[b])
    load("o0", outputs[0].at[:, own_k], wo.at[0, y, c], local_sem.at[2])
    load("docs", docs, docs_in, local_sem.at[3])
    load("kv1", keyvals[1], kvin.at[1], local_sem.at[4])
    load("q1", queries[1].at[own_k, :], wq.at[1, y, c], local_sem.at[5])
    load("o1", outputs[1].at[:, own_k], wo.at[1, y, c], local_sem.at[6])

    pl.semaphore_wait(barrier, len(greeted))

    def swap(n, src, dst):
        send(src, dst, swap_ss.at[n], swap_rs.at[n], mate)

    def swapped(n, dst):
        landed(dst, swap_ss.at[n], swap_rs.at[n])

    swap(0, queries[0].at[mate_k, :], wq.at[0, y, c])
    send(tokens.at[:, quarter(z, 1 - x_hi)], xs.at[0, z, x_hi], one_ss.at[0], one_rs.at[0], across)

    eye = (
        lax.broadcasted_iota(jnp.int32, (PIECE, PIECE), 0)
        == lax.broadcasted_iota(jnp.int32, (PIECE, PIECE), 1)
    ).astype(BF16)

    def turn_keyvals(layer):
        loads[f"kv{layer}"].wait()
        for half in range(2):
            kvt[layer, half] = dot_nt(eye, kvin[layer, half * WIDE : (half + 1) * WIDE, :]).astype(BF16)
        wkv[layer, y, c] = kvt[layer, c]
        swap(4 + layer, kvt.at[layer, 1 - c], wkv.at[layer, y, c])

    def ring_step(step, slot, me, n, peers, reach, ss, rs):
        for way in range(2):
            sign = 1 if way == 0 else n - 1
            block = (me + (n - sign) * (step - 1)) % n
            if 1 < step <= reach[way] + 1:
                landed(slot(block), ss.at[way, step - 2], rs.at[way, step - 2])
            if step <= reach[way]:
                ref = slot(block)
                send(ref, ref, ss.at[way, step - 1], rs.at[way, step - 1], peers[way])

    def query_step(layer, step):
        if step == 1:
            loads[f"q{layer}"].wait()
        for lane in range(2):
            head = c if lane == 0 else 1 - c
            if step == 1 and lane == 1:
                swapped(2 * layer, wq.at[layer, y, 1 - c])
            unit = 5 * layer + lane
            ring_step(step, lambda b: wq.at[layer, b, head], y, ny, y_next, REACH[lane], y_ss.at[unit], y_rs.at[unit])
        if step == 1:
            swapped(4 + layer, wkv.at[layer, y, 1 - c])
        unit = 5 * layer + 2
        ring_step(step, lambda b: wkv.at[layer, b], y, ny, y_next, REACH[layer], y_ss.at[unit], y_rs.at[unit])

    def output_step(layer, step):
        if step == 1:
            loads[f"o{layer}"].wait()
        for lane in range(2):
            head = c if lane == 0 else 1 - c
            if step == 1 and lane == 1:
                swapped(2 * layer + 1, wo.at[layer, y, 1 - c])
            unit = 5 * layer + 3 + lane
            ring_step(step, lambda b: wo.at[layer, b, head], y, ny, y_next, REACH[lane], y_ss.at[unit], y_rs.at[unit])

    def token_step(step):
        if step == 1:
            landed(xs.at[0, z, 1 - x_hi], one_ss.at[0], one_rs.at[0])
        ring_step(step, lambda b: xs.at[0, b, 1 - x_hi], z, nz, z_next, REACH[0], tok_ss, tok_rs)

    turn_keyvals(0)
    swap(1, outputs[0].at[:, mate_k], wo.at[0, y, c])
    query_step(0, 1)
    token_step(1)
    swap(2, queries[1].at[mate_k, :], wq.at[1, y, c])
    swap(3, outputs[1].at[:, mate_k], wo.at[1, y, c])
    turn_keyvals(1)

    loads["docs"].wait()
    doc_row = jnp.broadcast_to(docs_in[pl.ds(inst, 1), :], (ROWS, ROWS)).astype(F32)
    place_t = lax.broadcasted_iota(jnp.int32, (ROWS, ROWS), 0)
    place_s = lax.broadcasted_iota(jnp.int32, (ROWS, ROWS), 1)
    doc_col = dot_nt((place_t == place_s).astype(BF16), doc_row.astype(BF16))
    allowed = (doc_col == doc_row) & (place_s <= place_t)
    mask[...] = jnp.zeros_like(mask)
    mask[:, :ROWS] = jnp.where(allowed, 1.0, 0.0)
    tail_pad[...] = jnp.zeros_like(tail_pad)

    for b in range(nz):
        loads[("x", b)].wait()
    for step in range(2, 6):
        query_step(0, step)
        token_step(step)
    output_step(0, 1)

    lane_at = lax.broadcasted_iota(jnp.int32, (ROWS, HEAD), 1)
    select = (
        lax.broadcasted_iota(jnp.int32, (PIECE, HEAD), 0)
        == lax.broadcasted_iota(jnp.int32, (PIECE, HEAD), 1)
    ).astype(BF16)

    def pack(ref, q, tail, squares):
        high = squares.astype(BF16).astype(F32)
        low = squares - high
        tail = jnp.where(lane_at < PIECE, tail, jnp.where(lane_at == PIECE, high, 0.0))
        tail = jnp.where(lane_at == PIECE + 1, low, tail)
        ref[:, :HEAD] = q.astype(BF16)
        ref[:, HEAD:] = tail.astype(BF16)

    def squares_of(tail):
        return jnp.sum(jnp.where(lane_at < PIECE, 0.0, tail), axis=1, keepdims=True)

    def project(layer, first, last):
        def body(b, carry):
            x = xs[layer, b].reshape(2 * ROWS, WIDE)
            w = jnp.concatenate([wq[layer, b, 0], wq[layer, b, 1]], axis=1)
            q = jnp.dot(x, w, preferred_element_type=F32).reshape(2, ROWS, WIDE)
            xf = x.astype(F32)
            sq = (xf[:, :HEAD] * xf[:, :HEAD] + xf[:, HEAD:] * xf[:, HEAD:]).reshape(2, ROWS, HEAD)
            ass[...] += sq
            for h in range(2):
                aq[h] += q[:, :, h * HEAD : (h + 1) * HEAD]
                akv[h, :, :, :PIECE] += dot_nt(x, wkv[layer, b, h]).reshape(2, ROWS, PIECE)
            return carry

        lax.fori_loop(first, last, body, 0)

    def heads(layer, beside_step):
        aq[...] = jnp.zeros_like(aq)
        akv[...] = jnp.zeros_like(akv)
        ass[...] = jnp.zeros_like(ass)
        project(layer, 0, nz)
        for k in (1 - x_hi, x_hi):
            squares = jnp.sum(ass[k], axis=1, keepdims=True)
            pack(near_s.at[layer, k], aq[1 - c, k], akv[1 - c, k], squares)
            send(near_s.at[layer, k], near_r.at[layer, k], near_ss.at[layer, k], near_rs.at[layer, k], mate)
        beside_step(2)

        def chip_sum(k):
            landed(near_r.at[layer, k], near_ss.at[layer, k], near_rs.at[layer, k])
            squares = jnp.sum(ass[k], axis=1, keepdims=True)
            other = near_r[layer, k].astype(F32)
            tail = jnp.where(lane_at < PIECE, akv[c, k], jnp.where(lane_at == PIECE, squares, 0.0))
            return aq[c, k] + other[:, :HEAD], tail + other[:, HEAD:]

        q, tail = chip_sum(1 - x_hi)
        pack(far_s.at[layer], q, tail, squares_of(tail))
        send(far_s.at[layer], far_r.at[layer], far_ss.at[layer], far_rs.at[layer], across)
        beside_step(3)
        q, tail = chip_sum(x_hi)
        landed(far_r.at[layer], far_ss.at[layer], far_rs.at[layer])
        other = far_r[layer].astype(F32)
        q = q + other[:, :HEAD]
        tail = tail + other[:, HEAD:]
        scale = lax.rsqrt(squares_of(tail) * (1.0 / model) + 1e-06)
        q = (q * scale * HEAD**-0.5).astype(BF16)
        tail_pad[:ROWS, :] = jnp.where(lane_at < PIECE, tail * scale, 0.0).astype(BF16)
        kvs[layer, piece] = dot_nt(select, tail_pad[...]).astype(BF16)
        for n, peer in enumerate(sharers):
            ref = kvs.at[layer, piece]
            send(ref, ref, kv_ss.at[layer, n], kv_rs.at[layer, piece], peer)
        beside_step(4)
        for o in range(1, GROUP):
            p = (piece + o) % GROUP
            landed(kvs.at[layer, p], kv_ss.at[layer, 0], kv_rs.at[layer, p])
        keys = kvs[layer, 0:4].reshape(HEAD, WIDE)
        values = kvs[layer, 4:8].reshape(HEAD, WIDE)
        scores = jnp.dot(q, keys, preferred_element_type=F32)
        scores = jnp.where(mask[...] > 0.5, scores, -1e30)
        top = jnp.max(scores, axis=1, keepdims=True)
        weights = jnp.exp(scores - top)
        probs = (weights / jnp.sum(weights, axis=1, keepdims=True)).astype(BF16)
        ctx[layer, x_hi, c] = dot_nt(probs, values).astype(BF16)
        ref = ctx.at[layer, x_hi, c]
        slot = 2 * x_hi + c
        for n, peer in enumerate((across, across_mate, mate)):
            send(ref, ref, ctx_ss.at[layer, n], ctx_rs.at[layer, slot], peer)
        beside_step(5)
        for other_slot in (2 * x_hi + 1 - c, 2 * (1 - x_hi) + c, 2 * (1 - x_hi) + 1 - c):
            landed(ctx.at[layer, other_slot // 2, other_slot % 2], ctx_ss.at[layer, 0], ctx_rs.at[layer, other_slot])

    def reduce(layer, beside_step):
        ks = (1 - x_lo, x_lo)

        def product(b):
            left = jnp.concatenate([ctx[layer, :, 0].reshape(2 * ROWS, HEAD), ctx[layer, :, 1].reshape(2 * ROWS, HEAD)], axis=1)
            right = wo[layer, b].reshape(2 * HEAD, WIDE)
            pbuf[b] = jnp.dot(left, right, preferred_element_type=F32).reshape(2, ROWS, WIDE)

        def hop(lane, way, distance):
            b = (z + (distance if way == 0 else nz - distance)) % nz
            value = pbuf[b, ks[lane]]
            if distance < REACH[lane][way]:
                landed(rs_r.at[layer, lane, way, distance], z_ss.at[layer, lane, way, distance], z_rs.at[layer, lane, way, distance])
                value = value + rs_r[layer, lane, way, distance].astype(F32)
            if distance == 0:
                return value
            rs_s[layer, lane, way, distance - 1] = value.astype(BF16)
            send(
                rs_s.at[layer, lane, way, distance - 1],
                rs_r.at[layer, lane, way, distance - 1],
                z_ss.at[layer, lane, way, distance - 1],
                z_rs.at[layer, lane, way, distance - 1],
                z_next[way],
            )

        product((z + 4) % nz)
        hop(0, 0, 4)
        hop(1, 1, 4)

        def rest(j, carry):
            product((z + 5 + j) % nz)
            return carry

        lax.fori_loop(0, nz - 1, rest, 0)
        hop(1, 0, 3)
        hop(0, 1, 3)
        beside_step(1)
        hop(0, 0, 3)
        hop(1, 1, 3)
        for distance in (2, 1):
            hop(1, 0, distance)
            hop(0, 1, distance)
            hop(0, 0, distance)
            hop(1, 1, distance)
            beside_step(4 - distance)

        def collected(lane):
            total = hop(lane, 0, 0)
            landed(rs_r.at[layer, lane, 1, 0], z_ss.at[layer, lane, 1, 0], z_rs.at[layer, lane, 1, 0])
            return total + rs_r[layer, lane, 1, 0].astype(F32)

        half_s[layer] = collected(0).astype(BF16)
        send(half_s.at[layer], half_r.at[layer], half_ss.at[layer], half_rs.at[layer], beside)
        mine = collected(1)
        beside_step(4)
        landed(half_r.at[layer], half_ss.at[layer], half_rs.at[layer])
        mine = mine + half_r[layer].astype(F32)
        return (xs[layer, z, x_lo].astype(F32) + mine).astype(BF16)

    def nothing(step):
        pass

    heads(0, lambda step: output_step(0, step))
    middle = reduce(0, lambda step: query_step(1, step))
    xs[1, z, x_lo] = middle
    ref = xs.at[1, z, x_lo]
    send(ref, ref, one_ss.at[1], one_rs.at[1], beside)
    query_step(1, 5)
    for step in range(1, 6):
        for lane in range(2):
            k = x_lo if lane == 0 else 1 - x_lo
            if step == 1 and lane == 1:
                landed(xs.at[1, z, k], one_ss.at[1], one_rs.at[1])
            ring_step(step, lambda b: xs.at[1, b, k], z, nz, z_next, REACH[lane], ag_ss.at[lane], ag_rs.at[lane])
        output_step(1, step)
    heads(1, nothing)
    fin[...] = reduce(1, nothing)
    send(fin, out, one_ss.at[2], one_rs.at[2], goal)
    for move in sent:
        move.wait_send()
    landed(out, one_ss.at[2], one_rs.at[2])


def solution(mesh):
    ny, nz = mesh.shape["inst"] // 2, mesh.shape["tp"] // 4

    def shards(*operands):
        dma = pltpu.SemaphoreType.DMA
        anywhere = pl.BlockSpec(memory_space=pl.ANY)
        vmem = pltpu.VMEM
        return pl.pallas_call(
            functools.partial(kernel, ny, nz),
            out_shape=jax.ShapeDtypeStruct((ROWS, WIDE), BF16),
            in_specs=[anywhere] * 8,
            out_specs=anywhere,
            scratch_shapes=[
                vmem((2, ny, 2, WIDE, HEAD), BF16),
                vmem((2, ny, 2, PIECE, WIDE), BF16),
                vmem((2, ny, 2, HEAD, WIDE), BF16),
                vmem((2, 2 * WIDE, PIECE), BF16),
                vmem((2, 2, PIECE, WIDE), BF16),
                vmem((2 * ny, ROWS), jnp.int32),
                vmem((ROWS, WIDE), F32),
                vmem((2, nz, 2, ROWS, WIDE), BF16),
                vmem((2, 2, ROWS, HEAD), F32),
                vmem((2, 2, ROWS, HEAD), F32),
                vmem((2, ROWS, HEAD), F32),
                vmem((2, 2, ROWS, WIDE), BF16),
                vmem((2, 2, ROWS, WIDE), BF16),
                vmem((2, ROWS, WIDE), BF16),
                vmem((2, ROWS, WIDE), BF16),
                vmem((WIDE, HEAD), BF16),
                vmem((2, GROUP, PIECE, WIDE), BF16),
                vmem((2, 2, 2, ROWS, HEAD), BF16),
                vmem((nz, 2, ROWS, WIDE), F32),
                vmem((2, 2, 2, 4, ROWS, WIDE), BF16),
                vmem((2, 2, 2, 4, ROWS, WIDE), BF16),
                vmem((2, ROWS, WIDE), BF16),
                vmem((2, ROWS, WIDE), BF16),
                vmem((ROWS, WIDE), BF16),
                dma((7,)),
                dma((nz,)),
                dma((6,)),
                dma((6,)),
                dma((10, 2, 4)),
                dma((10, 2, 4)),
                dma((2, 4)),
                dma((2, 4)),
                dma((2, 2)),
                dma((2, 2)),
                dma((2,)),
                dma((2,)),
                dma((2, GROUP)),
                dma((2, GROUP)),
                dma((2, 3)),
                dma((2, 4)),
                dma((2, 2, 2, 4)),
                dma((2, 2, 2, 4)),
                dma((2,)),
                dma((2,)),
                dma((2, 2, 4)),
                dma((2, 2, 4)),
                dma((3,)),
                dma((3,)),
            ],
            compiler_params=pltpu.CompilerParams(
                collective_id=0,
                has_side_effects=True,
                vmem_limit_bytes=40 * 1024 * 1024,
            ),
            cost_estimate=pl.CostEstimate(
                flops=2_000_000_000, bytes_accessed=10_000_000, transcendentals=51200
            ),
        )(*operands)

    placed = (
        P("inst", None),
        P(),
        P("inst", "tp"),
        P("inst", "tp"),
        P("tp", "inst"),
        P("inst", "tp"),
        P("inst", "tp"),
        P("tp", "inst"),
    )
    return jax.shard_map(
        shards, mesh=mesh, in_specs=placed, out_specs=P("inst", "tp"), check_vma=False
    )
```

```python
import functools

import jax
import jax.numpy as jnp
from jax import lax
from jax.experimental import pallas as pl
from jax.experimental.pallas import tpu as pltpu
from jax.sharding import PartitionSpec as P

MESH = pl.DeviceIdType.MESH
F32 = jnp.float32
BF16 = jnp.bfloat16
NT = (((1,), (1,)), ((), ()))
ROWS = 160
HEAD = 128
PIECE = 32
WIDE = 256
GROUP = 8
REACH = ((4, 3), (3, 4))


def dot_nt(left, right):
    return lax.dot_general(left, right, NT, preferred_element_type=F32)


def kernel(
    ny,
    nz,
    tokens,
    docs,
    query_one,
    keyval_one,
    output_one,
    query_two,
    keyval_two,
    output_two,
    out,
    wq,
    wkv,
    wo,
    docs_in,
    mask,
    xs,
    xs_two,
    aq,
    akv,
    ass,
    near_s,
    near_r,
    far_s,
    far_r,
    tail_pad,
    kvs,
    ctx,
    pbuf,
    rs_s,
    rs_r,
    fin,
    local_sem,
    xlocal_sem,
    swap_ss,
    swap_rs,
    y_ss,
    y_rs,
    tok_ss,
    tok_rs,
    near_ss,
    near_rs,
    far_ss,
    far_rs,
    kv_ss,
    kv_rs,
    ctx_ss,
    ctx_rs,
    z_ss,
    z_rs,
    ag_ss,
    ag_rs,
    one_ss,
    one_rs,
    fin_ss,
    fin_rs,
):
    inst = lax.axis_index("inst")
    rank = lax.axis_index("tp")
    ninst, nrank = 2 * ny, 4 * nz
    y, x_hi = inst // 2, inst % 2
    z, x_lo, c = rank // 4, rank // 2 % 2, rank % 2
    piece = rank % GROUP
    model = ny * 2 * 512

    mate = (inst, rank + 1 - 2 * c)
    across = (inst + 1 - 2 * x_hi, rank)
    beside = (inst, rank + 2 - 4 * x_lo)
    y_next = (((inst + 2) % ninst, rank), ((inst + ninst - 2) % ninst, rank))
    z_next = ((inst, (rank + 4) % nrank), (inst, (rank + nrank - 4) % nrank))
    beside_mate = (inst, rank + 3 - 4 * x_lo - 2 * c)
    goals = [((2 * y + k + 1) % ninst, 4 * z + 2 * x_hi + c) for k in range(2)]
    origin_inst = (inst + ninst - 1) % ninst // 2 * 2 + x_lo
    origins = [(origin_inst, 4 * z + 2 * s + c) for s in range(2)]
    stays = x_hi * x_lo

    group_base = rank // GROUP * GROUP
    sharers = [(inst, group_base + (piece + o) % GROUP) for o in range(1, GROUP)]
    other_z = (inst, (rank + nrank + 4 * (2 * (z % 2) - 1)) % nrank)

    barrier = pltpu.get_barrier_semaphore()
    greeted = sharers + [other_z, y_next[0], y_next[1], across, origins[0]]
    for peer in greeted:
        pl.semaphore_signal(barrier, inc=1, device_id=peer, device_id_type=MESH)

    @pl.when(stays == 0)
    def _():
        pl.semaphore_signal(barrier, inc=1, device_id=origins[1], device_id_type=MESH)

    sent = []

    def copy(src, dst, send, recv, peer):
        return pltpu.make_async_remote_copy(
            src_ref=src,
            dst_ref=dst,
            send_sem=send,
            recv_sem=recv,
            device_id=peer,
            device_id_type=MESH,
        )

    def send(*args):
        move = copy(*args)
        move.start()
        sent.append(move)

    def landed(dst, send_sem, recv_sem):
        copy(dst, dst, send_sem, recv_sem, mate).wait_recv()

    queries = (query_one, query_two)
    keyvals = (keyval_one, keyval_two)
    outputs = (output_one, output_two)
    loads = {}

    def load(name, src, dst, sem):
        loads[name] = pltpu.make_async_copy(src, dst, sem)
        loads[name].start()

    def quarter(block, hi):
        return pl.ds(pl.multiple_of((2 * block + hi) * 512 + c * WIDE, WIDE), WIDE)

    own_k = pl.ds(pl.multiple_of(c * WIDE, WIDE), WIDE)
    mate_k = pl.ds(pl.multiple_of((1 - c) * WIDE, WIDE), WIDE)
    own_part = pl.ds(pl.multiple_of((2 * c + x_lo) * HEAD, HEAD), HEAD)
    load("kv0", keyvals[0].at[:, own_k], wkv.at[0, y, c], local_sem.at[0])
    load("q0", queries[0].at[own_k, :], wq.at[0, y, c], local_sem.at[1])
    for b in range(nz):
        load(("x", b), tokens.at[:, quarter(b, x_hi)], xs.at[b, x_hi], xlocal_sem.at[b])
    load("o0", outputs[0].at[:, own_part], wo.at[0, y, x_lo, c], local_sem.at[2])
    load("docs", docs, docs_in, local_sem.at[3])
    load("kv1", keyvals[1].at[:, own_k], wkv.at[1, y, c], local_sem.at[4])
    load("q1", queries[1].at[own_k, :], wq.at[1, y, c], local_sem.at[5])
    load("o1", outputs[1].at[:, own_part], wo.at[1, y, x_lo, c], local_sem.at[6])

    pl.semaphore_wait(barrier, len(greeted) + 1 - stays)

    def swap(layer, n, src, dst, peer):
        send(src, dst, swap_ss.at[layer, n], swap_rs.at[layer, n], peer)

    def swapped(layer, n, dst):
        landed(dst, swap_ss.at[layer, n], swap_rs.at[layer, n])

    def swap_query(layer):
        swap(layer, 0, queries[layer].at[mate_k, :], wq.at[layer, y, c], mate)
        swap(layer, 1, keyvals[layer].at[:, mate_k], wkv.at[layer, y, c], mate)

    def part(lo, core):
        return pl.ds(pl.multiple_of((2 * core + lo) * HEAD, HEAD), HEAD)

    def swap_output(layer):
        dst = wo.at[layer, y, x_lo, c]
        swap(layer, 2, outputs[layer].at[:, part(x_lo, 1 - c)], dst, mate)
        swap(layer, 3, outputs[layer].at[:, part(1 - x_lo, c)], dst, beside)
        swap(layer, 4, outputs[layer].at[:, part(1 - x_lo, 1 - c)], dst, beside_mate)

    swap_query(0)
    send(tokens.at[:, quarter(z, 1 - x_hi)], xs.at[z, x_hi], one_ss.at[0], one_rs.at[0], across)

    def ring_step(step, slot, me, n, peers, reach, ss, rs):
        for way in range(2):
            sign = 1 if way == 0 else n - 1
            block = (me + (n - sign) * (step - 1)) % n
            if 1 < step <= reach[way] + 1:
                landed(slot(block), ss.at[way, step - 2], rs.at[way, step - 2])
            if step <= reach[way]:
                ref = slot(block)
                send(ref, ref, ss.at[way, step - 1], rs.at[way, step - 1], peers[way])

    def query_step(layer, step):
        if step == 1:
            loads[f"q{layer}"].wait()
        for lane in range(2):
            head = c if lane == 0 else 1 - c
            if step == 1 and lane == 1:
                swapped(layer, 0, wq.at[layer, y, 1 - c])
            unit = 5 * layer + lane
            ring_step(step, lambda b: wq.at[layer, b, head], y, ny, y_next, REACH[lane], y_ss.at[unit], y_rs.at[unit])
        if step == 1:
            loads[f"kv{layer}"].wait()
            swapped(layer, 1, wkv.at[layer, y, 1 - c])
        unit = 5 * layer + 2
        ring_step(step, lambda b: wkv.at[layer, b], y, ny, y_next, REACH[layer], y_ss.at[unit], y_rs.at[unit])

    def output_step(layer, step):
        if step == 1:
            loads[f"o{layer}"].wait()
        for lane in range(2):
            lo = x_lo if lane == 0 else 1 - x_lo
            if step == 1 and lane == 0:
                swapped(layer, 2, wo.at[layer, y, x_lo, 1 - c])
            if step == 1 and lane == 1:
                swapped(layer, 3, wo.at[layer, y, 1 - x_lo, c])
                swapped(layer, 4, wo.at[layer, y, 1 - x_lo, 1 - c])
            unit = 5 * layer + 3 + lane
            ring_step(step, lambda b: wo.at[layer, b, lo], y, ny, y_next, REACH[lane], y_ss.at[unit], y_rs.at[unit])

    def token_step(step):
        if step == 1:
            landed(xs.at[z, 1 - x_hi], one_ss.at[0], one_rs.at[0])
        ring_step(step, lambda b: xs.at[b, 1 - x_hi], z, nz, z_next, REACH[0], tok_ss, tok_rs)

    query_step(0, 1)
    swap_output(0)
    token_step(1)
    swap_query(1)
    swap_output(1)

    loads["docs"].wait()
    doc_row = jnp.broadcast_to(docs_in[pl.ds(inst, 1), :], (ROWS, ROWS)).astype(F32)
    place_t = lax.broadcasted_iota(jnp.int32, (ROWS, ROWS), 0)
    place_s = lax.broadcasted_iota(jnp.int32, (ROWS, ROWS), 1)
    doc_col = dot_nt((place_t == place_s).astype(BF16), doc_row.astype(BF16))
    allowed = (doc_col == doc_row) & (place_s <= place_t)
    mask[...] = jnp.zeros_like(mask)
    mask[:, :ROWS] = jnp.where(allowed, 1.0, 0.0)
    tail_pad[...] = jnp.zeros_like(tail_pad)

    lane_at = lax.broadcasted_iota(jnp.int32, (ROWS, HEAD), 1)
    select = (
        lax.broadcasted_iota(jnp.int32, (PIECE, HEAD), 0)
        == lax.broadcasted_iota(jnp.int32, (PIECE, HEAD), 1)
    ).astype(BF16)

    def pack(ref, q, tail, squares):
        high = squares.astype(BF16).astype(F32)
        low = squares - high
        tail = jnp.where(lane_at < PIECE, tail, jnp.where(lane_at == PIECE, high, 0.0))
        tail = jnp.where(lane_at == PIECE + 1, low, tail)
        ref[:, :HEAD] = q.astype(BF16)
        ref[:, HEAD:] = tail.astype(BF16)

    def squares_of(tail):
        return jnp.sum(jnp.where(lane_at < PIECE, 0.0, tail), axis=1, keepdims=True)

    def clear():
        aq[...] = jnp.zeros_like(aq)
        akv[...] = jnp.zeros_like(akv)
        ass[...] = jnp.zeros_like(ass)

    def project(layer, first, count):
        def body(j, carry):
            b = (first + j) % nz
            if layer == 0:
                x = xs[b].reshape(2 * ROWS, WIDE)
            else:
                x = jnp.concatenate([xs_two[b, 0].reshape(2 * ROWS, HEAD), xs_two[b, 1].reshape(2 * ROWS, HEAD)], axis=1)
            w = jnp.concatenate([wq[layer, b, 0], wq[layer, b, 1]], axis=1)
            q = jnp.dot(x, w, preferred_element_type=F32).reshape(2, ROWS, WIDE)
            xf = x.astype(F32)
            sq = (xf[:, :HEAD] * xf[:, :HEAD] + xf[:, HEAD:] * xf[:, HEAD:]).reshape(2, ROWS, HEAD)
            ass[...] += sq
            for h in range(2):
                aq[h] += q[:, :, h * HEAD : (h + 1) * HEAD]
                akv[h, :, :, :PIECE] += dot_nt(x, wkv[layer, b, h]).reshape(2, ROWS, PIECE)
            return carry

        lax.fori_loop(0, count, body, 0)

    def heads(layer, beside_step):
        for k in (1 - x_hi, x_hi):
            squares = jnp.sum(ass[k], axis=1, keepdims=True)
            pack(near_s.at[layer, k], aq[1 - c, k], akv[1 - c, k], squares)
            send(near_s.at[layer, k], near_r.at[layer, k], near_ss.at[layer, k], near_rs.at[layer, k], mate)
        beside_step(2)

        def chip_sum(k):
            landed(near_r.at[layer, k], near_ss.at[layer, k], near_rs.at[layer, k])
            squares = jnp.sum(ass[k], axis=1, keepdims=True)
            other = near_r[layer, k].astype(F32)
            tail = jnp.where(lane_at < PIECE, akv[c, k], jnp.where(lane_at == PIECE, squares, 0.0))
            return aq[c, k] + other[:, :HEAD], tail + other[:, HEAD:]

        q, tail = chip_sum(1 - x_hi)
        pack(far_s.at[layer], q, tail, squares_of(tail))
        send(far_s.at[layer], far_r.at[layer], far_ss.at[layer], far_rs.at[layer], across)
        beside_step(3)
        q, tail = chip_sum(x_hi)
        landed(far_r.at[layer], far_ss.at[layer], far_rs.at[layer])
        other = far_r[layer].astype(F32)
        q = q + other[:, :HEAD]
        tail = tail + other[:, HEAD:]
        scale = lax.rsqrt(squares_of(tail) * (1.0 / model) + 1e-06)
        q = (q * scale * HEAD**-0.5).astype(BF16)
        tail_pad[:ROWS, :] = jnp.where(lane_at < PIECE, tail * scale, 0.0).astype(BF16)
        kvs[layer, piece] = dot_nt(select, tail_pad[...]).astype(BF16)
        for n, peer in enumerate(sharers):
            ref = kvs.at[layer, piece]
            send(ref, ref, kv_ss.at[layer, n], kv_rs.at[layer, piece], peer)
        beside_step(4)
        for o in range(1, GROUP):
            p = (piece + o) % GROUP
            landed(kvs.at[layer, p], kv_ss.at[layer, 0], kv_rs.at[layer, p])
        keys = kvs[layer, 0:4].reshape(HEAD, WIDE)
        values = kvs[layer, 4:8].reshape(HEAD, WIDE)
        scores = jnp.dot(q, keys, preferred_element_type=F32)
        scores = jnp.where(mask[...] > 0.5, scores, -1e30)
        top = jnp.max(scores, axis=1, keepdims=True)
        weights = jnp.exp(scores - top)
        probs = (weights / jnp.sum(weights, axis=1, keepdims=True)).astype(BF16)
        place = 2 * x_lo + c
        ctx[layer, x_hi, place] = dot_nt(probs, values).astype(BF16)
        spread(layer, x_hi, (across, mate, beside, beside_mate), 0)
        beside_step(5)

    def spread(layer, k, peers, first):
        ref = ctx.at[layer, k, 2 * x_lo + c]
        for n, peer in enumerate(peers):
            send(ref, ref, ctx_ss.at[layer, first + n], ctx_rs.at[layer, k, 2 * x_lo + c], peer)

    def spread_in(layer, k, place):
        landed(ctx.at[layer, k, place], ctx_ss.at[layer, 0], ctx_rs.at[layer, k, place])

    def reduce(layer, beside_step):
        ks = (x_hi, 1 - x_hi)
        others = (2 * x_lo + 1 - c, 2 * (1 - x_lo) + c, 2 * (1 - x_lo) + 1 - c)

        def products(k):
            left = jnp.concatenate([ctx[layer, k, n] for n in range(4)], axis=1)

            def body(j, carry):
                b = (z + 4 + j) % nz
                right = wo[layer, b].reshape(4 * HEAD, HEAD)
                pbuf[b, k] = jnp.dot(left, right, preferred_element_type=F32)
                return carry

            lax.fori_loop(0, nz, body, 0)

        def hop(lane, way, distance):
            b = (z + (distance if way == 0 else nz - distance)) % nz
            value = pbuf[b, ks[lane]]
            if distance < REACH[lane][way]:
                landed(rs_r.at[layer, lane, way, distance], z_ss.at[layer, lane, way, distance], z_rs.at[layer, lane, way, distance])
                value = value + rs_r[layer, lane, way, distance].astype(F32)
            if distance == 0:
                return value
            rs_s[layer, lane, way, distance - 1] = value.astype(BF16)
            send(
                rs_s.at[layer, lane, way, distance - 1],
                rs_r.at[layer, lane, way, distance - 1],
                z_ss.at[layer, lane, way, distance - 1],
                z_rs.at[layer, lane, way, distance - 1],
                z_next[way],
            )

        spread_in(layer, 1 - x_hi, 2 * x_lo + c)
        spread(layer, 1 - x_hi, (mate, beside, beside_mate), 4)
        for place in others:
            spread_in(layer, x_hi, place)
        products(x_hi)
        hop(0, 0, 4)
        hop(0, 1, 3)
        beside_step(1)
        for place in others:
            spread_in(layer, 1 - x_hi, place)
        products(1 - x_hi)
        hop(1, 1, 4)
        hop(1, 0, 3)
        hop(0, 0, 3)
        hop(0, 1, 2)
        beside_step(2)
        hop(1, 1, 3)
        hop(1, 0, 2)
        hop(0, 0, 2)
        hop(0, 1, 1)
        beside_step(3)
        hop(1, 1, 2)
        hop(1, 0, 1)
        hop(0, 0, 1)
        beside_step(4)
        hop(1, 1, 1)

        def collected(lane):
            total = hop(lane, 0, 0)
            landed(rs_r.at[layer, lane, 1, 0], z_ss.at[layer, lane, 1, 0], z_rs.at[layer, lane, 1, 0])
            total = total + rs_r[layer, lane, 1, 0].astype(F32)
            k = ks[lane]
            if layer == 0:
                old = xs[z, k, :, pl.ds(pl.multiple_of(x_lo * HEAD, HEAD), HEAD)]
            else:
                old = xs_two[z, x_lo, k]
            return (old.astype(F32) + total).astype(BF16)

        return collected

    def nothing(step):
        pass

    clear()
    for b in range(nz):
        loads[("x", b)].wait()
    query_step(0, 2)
    token_step(2)
    query_step(0, 3)
    token_step(3)
    token_step(4)
    query_step(0, 4)
    token_step(5)
    output_step(0, 1)
    project(0, y + ny - 3, ny - 1)
    query_step(0, 5)
    project(0, y + 4, 1)
    heads(0, lambda step: output_step(0, step))
    collected = reduce(0, lambda step: query_step(1, step))
    for lane in range(2):
        k = x_hi if lane == 0 else 1 - x_hi
        xs_two[z, x_lo, k] = collected(lane)
    ref = xs_two.at[z, x_lo]
    send(ref, ref, one_ss.at[1], one_rs.at[1], beside)
    for step in range(1, 6):
        for lane in range(2):
            half = x_lo if lane == 0 else 1 - x_lo
            if step == 1 and lane == 1:
                landed(xs_two.at[z, half], one_ss.at[1], one_rs.at[1])
            ring_step(step, lambda b: xs_two.at[b, half], z, nz, z_next, REACH[lane], ag_ss.at[lane], ag_rs.at[lane])
        if step == 1:
            query_step(1, 5)
            clear()
        output_step(1, step)
        if step == 4:
            project(1, z + nz - 3, nz - 1)
    project(1, z + 4, 1)
    heads(1, nothing)
    collected = reduce(1, nothing)
    for lane in range(2):
        k = x_hi if lane == 0 else 1 - x_hi
        fin[k] = collected(lane)
    own_half = pl.ds(pl.multiple_of(x_lo * HEAD, HEAD), HEAD)
    moves = [
        copy(fin.at[k], out.at[:, own_half], fin_ss.at[k], fin_rs.at[x_lo], goals[k]) for k in range(2)
    ]
    moves[1].start()

    @pl.when(stays == 0)
    def _():
        moves[0].start()
        moves[0].wait_send()

    @pl.when(stays == 1)
    def _():
        keep = pltpu.make_async_copy(fin.at[0], out.at[:, own_half], local_sem.at[0])
        keep.start()
        keep.wait()

    moves[1].wait_send()
    for move in sent:
        move.wait_send()
    landed(out.at[:, :HEAD], fin_ss.at[0], fin_rs.at[0])

    @pl.when(stays == 0)
    def _():
        landed(out.at[:, HEAD:], fin_ss.at[1], fin_rs.at[1])


def solution(mesh):
    ny, nz = mesh.shape["inst"] // 2, mesh.shape["tp"] // 4

    def shards(tokens, docs, q1, kv1, o1, q2, kv2, o2):
        operands = [pltpu.with_memory_space_constraint(a, pltpu.HBM) for a in (tokens, docs, q1, kv1.T, o1, q2, kv2.T, o2)]
        dma = pltpu.SemaphoreType.DMA
        anywhere = pl.BlockSpec(memory_space=pltpu.HBM)
        vmem = pltpu.VMEM
        return pl.pallas_call(
            functools.partial(kernel, ny, nz),
            out_shape=jax.ShapeDtypeStruct((ROWS, WIDE), BF16),
            in_specs=[anywhere] * 8,
            out_specs=anywhere,
            scratch_shapes=[
                vmem((2, ny, 2, WIDE, HEAD), BF16),
                vmem((2, ny, 2, PIECE, WIDE), BF16),
                vmem((2, ny, 2, 2, HEAD, HEAD), BF16),
                vmem((2 * ny, ROWS), jnp.int32),
                vmem((ROWS, WIDE), F32),
                vmem((nz, 2, ROWS, WIDE), BF16),
                vmem((nz, 2, 2, ROWS, HEAD), BF16),
                vmem((2, 2, ROWS, HEAD), F32),
                vmem((2, 2, ROWS, HEAD), F32),
                vmem((2, ROWS, HEAD), F32),
                vmem((2, 2, ROWS, WIDE), BF16),
                vmem((2, 2, ROWS, WIDE), BF16),
                vmem((2, ROWS, WIDE), BF16),
                vmem((2, ROWS, WIDE), BF16),
                vmem((WIDE, HEAD), BF16),
                vmem((2, GROUP, PIECE, WIDE), BF16),
                vmem((2, 2, 4, ROWS, HEAD), BF16),
                vmem((nz, 2, ROWS, HEAD), F32),
                vmem((2, 2, 2, 4, ROWS, HEAD), BF16),
                vmem((2, 2, 2, 4, ROWS, HEAD), BF16),
                vmem((2, ROWS, HEAD), BF16),
                dma((7,)),
                dma((nz,)),
                dma((2, 5)),
                dma((2, 5)),
                dma((10, 2, 4)),
                dma((10, 2, 4)),
                dma((2, 4)),
                dma((2, 4)),
                dma((2, 2)),
                dma((2, 2)),
                dma((2,)),
                dma((2,)),
                dma((2, GROUP)),
                dma((2, GROUP)),
                dma((2, 7)),
                dma((2, 2, 4)),
                dma((2, 2, 2, 4)),
                dma((2, 2, 2, 4)),
                dma((2, 2, 4)),
                dma((2, 2, 4)),
                dma((2,)),
                dma((2,)),
                dma((2,)),
                dma((2,)),
            ],
            compiler_params=pltpu.CompilerParams(
                collective_id=0,
                has_side_effects=True,
                vmem_limit_bytes=40 * 1024 * 1024,
            ),
            cost_estimate=pl.CostEstimate(
                flops=2_000_000_000, bytes_accessed=10_000_000, transcendentals=51200
            ),
        )(*operands)

    placed = (
        P("inst", None),
        P(),
        P("inst", "tp"),
        P("inst", "tp"),
        P("tp", "inst"),
        P("inst", "tp"),
        P("inst", "tp"),
        P("tp", "inst"),
    )
    return jax.shard_map(
        shards, mesh=mesh, in_specs=placed, out_specs=P("inst", "tp"), check_vma=False
    )
```

```python
import functools

import jax
import jax.numpy as jnp
from jax import lax
from jax.experimental import pallas as pl
from jax.experimental.pallas import tpu as pltpu
from jax.sharding import PartitionSpec as P

MESH = pl.DeviceIdType.MESH
F32 = jnp.float32
BF16 = jnp.bfloat16
NT = (((1,), (1,)), ((), ()))
ROWS = 160
HEAD = 128
PIECE = 32
WIDE = 256
GROUP = 8
REACH = ((4, 3), (3, 4))


def dot_nt(left, right):
    return lax.dot_general(left, right, NT, preferred_element_type=F32)


def kernel(
    ny,
    nz,
    tokens,
    docs,
    query_one,
    keyval_one,
    output_one,
    query_two,
    keyval_two,
    output_two,
    out,
    wq,
    wkv,
    wo,
    docs_in,
    mask,
    xs,
    xs_two,
    aq,
    akv,
    ass,
    near_s,
    near_r,
    far_s,
    far_r,
    tail_pad,
    kvs,
    ctx,
    pbuf,
    rs_s,
    rs_r,
    fin,
    local_sem,
    xlocal_sem,
    swap_ss,
    swap_rs,
    y_ss,
    y_rs,
    tok_ss,
    tok_rs,
    near_ss,
    near_rs,
    far_ss,
    far_rs,
    kv_ss,
    kv_rs,
    ctx_ss,
    ctx_rs,
    z_ss,
    z_rs,
    ag_ss,
    ag_rs,
    one_ss,
    one_rs,
    fin_ss,
    fin_rs,
):
    inst = lax.axis_index("inst")
    rank = lax.axis_index("tp")
    ninst, nrank = 2 * ny, 4 * nz
    y, x_hi = inst // 2, inst % 2
    z, x_lo, c = rank // 4, rank // 2 % 2, rank % 2
    piece = rank % GROUP
    model = ny * 2 * 512

    mate = (inst, rank + 1 - 2 * c)
    across = (inst + 1 - 2 * x_hi, rank)
    beside = (inst, rank + 2 - 4 * x_lo)
    y_next = (((inst + 2) % ninst, rank), ((inst + ninst - 2) % ninst, rank))
    z_next = ((inst, (rank + 4) % nrank), (inst, (rank + nrank - 4) % nrank))
    across_beside = (inst + 1 - 2 * x_hi, rank + 2 - 4 * x_lo)
    across_beside_mate = (inst + 1 - 2 * x_hi, rank + 3 - 4 * x_lo - 2 * c)
    beside_mate = (inst, rank + 3 - 4 * x_lo - 2 * c)
    goals = [((2 * y + k + 1) % ninst, 4 * z + 2 * x_hi + c) for k in range(2)]
    origin_inst = (inst + ninst - 1) % ninst // 2 * 2 + x_lo
    origins = [(origin_inst, 4 * z + 2 * s + c) for s in range(2)]
    stays = x_hi * x_lo

    group_base = rank // GROUP * GROUP
    sharers = [(inst, group_base + (piece + o) % GROUP) for o in range(1, GROUP)]
    other_rank = (rank + nrank + 4 * (2 * (z % 2) - 1)) % nrank
    other_z = (inst, other_rank)
    other_diagonal = (inst, other_rank + 2 - 4 * x_lo)
    z_second = ((inst, (rank + 8) % nrank), (inst, (rank + nrank - 8) % nrank))
    diagonal = tuple((inst, peer + 2 - 4 * x_lo) for _, peer in z_next)

    barrier = pltpu.get_barrier_semaphore()
    greeted = sharers + [other_z, other_diagonal, *z_second, *y_next, across, origins[0]]
    greeted += [across_beside, across_beside_mate]
    for peer in greeted:
        pl.semaphore_signal(barrier, inc=1, device_id=peer, device_id_type=MESH)

    @pl.when(stays == 0)
    def _():
        pl.semaphore_signal(barrier, inc=1, device_id=origins[1], device_id_type=MESH)

    sent = []

    def copy(src, dst, send, recv, peer):
        return pltpu.make_async_remote_copy(
            src_ref=src,
            dst_ref=dst,
            send_sem=send,
            recv_sem=recv,
            device_id=peer,
            device_id_type=MESH,
        )

    def send(*args):
        move = copy(*args)
        move.start()
        sent.append(move)

    def landed(dst, send_sem, recv_sem):
        copy(dst, dst, send_sem, recv_sem, mate).wait_recv()

    queries = (query_one, query_two)
    keyvals = (keyval_one, keyval_two)
    outputs = (output_one, output_two)
    loads = {}

    def load(name, src, dst, sem):
        loads[name] = pltpu.make_async_copy(src, dst, sem)
        loads[name].start()

    def quarter(block, hi):
        return pl.ds(pl.multiple_of((2 * block + hi) * 512 + c * WIDE, WIDE), WIDE)

    own_k = pl.ds(pl.multiple_of(c * WIDE, WIDE), WIDE)
    mate_k = pl.ds(pl.multiple_of((1 - c) * WIDE, WIDE), WIDE)
    own_part = pl.ds(pl.multiple_of((2 * c + x_lo) * HEAD, HEAD), HEAD)
    load("kv0", keyvals[0].at[:, own_k], wkv.at[0, y, c], local_sem.at[0])
    load("q0", queries[0].at[own_k, :], wq.at[0, y, c], local_sem.at[1])
    for b in range(nz):
        load(("x", b), tokens.at[:, quarter(b, x_hi)], xs.at[b, x_hi], xlocal_sem.at[b])
    load("o0", outputs[0].at[:, own_part], wo.at[0, y, x_lo, c], local_sem.at[2])
    load("docs", docs, docs_in, local_sem.at[3])
    load("kv1", keyvals[1].at[:, own_k], wkv.at[1, y, c], local_sem.at[4])
    load("q1", queries[1].at[own_k, :], wq.at[1, y, c], local_sem.at[5])
    load("o1", outputs[1].at[:, own_part], wo.at[1, y, x_lo, c], local_sem.at[6])

    pl.semaphore_wait(barrier, len(greeted) + 1 - stays)

    def swap(layer, n, src, dst, peer):
        send(src, dst, swap_ss.at[layer, n], swap_rs.at[layer, n], peer)

    def swapped(layer, n, dst):
        landed(dst, swap_ss.at[layer, n], swap_rs.at[layer, n])

    def swap_query(layer):
        swap(layer, 0, queries[layer].at[mate_k, :], wq.at[layer, y, c], mate)
        swap(layer, 1, keyvals[layer].at[:, mate_k], wkv.at[layer, y, c], mate)

    def part(lo, core):
        return pl.ds(pl.multiple_of((2 * core + lo) * HEAD, HEAD), HEAD)

    def swap_output(layer):
        dst = wo.at[layer, y, x_lo, c]
        swap(layer, 2, outputs[layer].at[:, part(x_lo, 1 - c)], dst, mate)
        swap(layer, 3, outputs[layer].at[:, part(1 - x_lo, c)], dst, beside)
        swap(layer, 4, outputs[layer].at[:, part(1 - x_lo, 1 - c)], dst, beside_mate)

    swap_query(0)
    token_rows = [pl.ds(lane * (ROWS // 2), ROWS // 2) for lane in range(2)]
    for lane, rows in enumerate(token_rows):
        src = tokens.at[rows, quarter(z, 1 - x_hi)]
        send(src, xs.at[z, x_hi, rows], one_ss.at[3 * lane], one_rs.at[3 * lane], across_beside)

    def ring_step(step, slot, me, n, peers, reach, ss, rs, opens=True):
        for way in range(2):
            sign = 1 if way == 0 else n - 1
            block = (me + (n - sign) * (step - 1)) % n
            if 1 < step <= reach[way] + 1:
                landed(slot(block), ss.at[way, step - 2], rs.at[way, step - 2])
            if step <= reach[way] and (opens or step > 1):
                ref = slot(block)
                send(ref, ref, ss.at[way, step - 1], rs.at[way, step - 1], peers[way])

    def query_step(layer, step):
        if step == 1:
            loads[f"q{layer}"].wait()
        for lane in range(4):
            head = c if lane < 2 else 1 - c
            if step == 1 and lane == 2:
                swapped(layer, 0, wq.at[layer, y, 1 - c])
            unit = 9 * layer + lane
            rows = pl.ds(lane % 2 * HEAD, HEAD)
            ring_step(
                step,
                lambda b: wq.at[layer, b, head, rows],
                y,
                ny,
                y_next,
                REACH[lane % 2],
                y_ss.at[unit],
                y_rs.at[unit],
            )
        if step == 1:
            loads[f"kv{layer}"].wait()
            swapped(layer, 1, wkv.at[layer, y, 1 - c])
        unit = 9 * layer + 4
        ring_step(step, lambda b: wkv.at[layer, b], y, ny, y_next, REACH[layer], y_ss.at[unit], y_rs.at[unit])

    def output_step(layer, step):
        if step == 1:
            loads[f"o{layer}"].wait()
        for lane in range(4):
            lo = x_lo if lane < 2 else 1 - x_lo
            core = c if lane % 2 == 0 else 1 - c
            if step == 1 and lane > 0:
                swapped(layer, 1 + lane, wo.at[layer, y, lo, core])
            unit = 9 * layer + 5 + lane
            ring_step(
                step,
                lambda b: wo.at[layer, b, lo, core],
                y,
                ny,
                y_next,
                REACH[lane % 2],
                y_ss.at[unit],
                y_rs.at[unit],
            )

    def token_part(b, lane):
        return xs.at[b, 1 - x_hi, token_rows[lane]]

    def token_block(way, distance):
        return (z + (nz - distance if way == 0 else distance)) % nz

    def token_send(lane, way, message, b, peers):
        ref = token_part(b, lane)
        send(ref, ref, tok_ss.at[lane, way, message], tok_rs.at[lane, way, message], peers[way])

    def token_landed(lane, way, distance):
        n = distance - 1
        landed(token_part(token_block(way, distance), lane), tok_ss.at[lane, way, n], tok_rs.at[lane, way, n])

    def token_open():
        for lane in range(2):
            landed(token_part(z, lane), one_ss.at[3 * lane], one_rs.at[3 * lane])
            for way in range(2):
                token_send(lane, way, 1, z, z_second)
            for way in range(2):
                token_send(lane, way, 0, z, z_next)

    def token_forward():
        for lane in range(2):
            for way in range(2):
                token_landed(lane, way, 2)
                b = token_block(way, 2)
                if way == lane:
                    token_send(lane, way, 3, b, z_second)
                token_send(lane, way, 2, b, z_next)

    def token_close():
        for lane in range(2):
            for way in range(2):
                token_landed(lane, way, 1)
                token_landed(lane, way, 3)
                if way == lane:
                    token_landed(lane, way, 4)

    query_step(0, 1)
    swap_output(0)
    token_open()
    swap_query(1)
    swap_output(1)

    loads["docs"].wait()
    doc_row = jnp.broadcast_to(docs_in[pl.ds(inst, 1), :], (ROWS, ROWS)).astype(F32)
    place_t = lax.broadcasted_iota(jnp.int32, (ROWS, ROWS), 0)
    place_s = lax.broadcasted_iota(jnp.int32, (ROWS, ROWS), 1)
    doc_col = dot_nt((place_t == place_s).astype(BF16), doc_row.astype(BF16))
    allowed = (doc_col == doc_row) & (place_s <= place_t)
    mask[...] = jnp.zeros_like(mask)
    mask[:, :ROWS] = jnp.where(allowed, 1.0, 0.0)
    tail_pad[...] = jnp.zeros_like(tail_pad)

    lane_at = lax.broadcasted_iota(jnp.int32, (ROWS, HEAD), 1)
    select = (
        lax.broadcasted_iota(jnp.int32, (PIECE, HEAD), 0)
        == lax.broadcasted_iota(jnp.int32, (PIECE, HEAD), 1)
    ).astype(BF16)

    def pack(ref, q, tail, squares):
        high = squares.astype(BF16).astype(F32)
        low = squares - high
        tail = jnp.where(lane_at < PIECE, tail, jnp.where(lane_at == PIECE, high, 0.0))
        tail = jnp.where(lane_at == PIECE + 1, low, tail)
        ref[:, :HEAD] = q.astype(BF16)
        ref[:, HEAD:] = tail.astype(BF16)

    def squares_of(tail):
        return jnp.sum(jnp.where(lane_at < PIECE, 0.0, tail), axis=1, keepdims=True)

    def clear():
        aq[...] = jnp.zeros_like(aq)
        akv[...] = jnp.zeros_like(akv)
        ass[...] = jnp.zeros_like(ass)

    def project(layer, first, count):
        def body(j, carry):
            b = (first + j) % nz
            if layer == 0:
                x = xs[b].reshape(2 * ROWS, WIDE)
            else:
                x = jnp.concatenate([xs_two[b, 0].reshape(2 * ROWS, HEAD), xs_two[b, 1].reshape(2 * ROWS, HEAD)], axis=1)
            w = jnp.concatenate([wq[layer, b, 0], wq[layer, b, 1]], axis=1)
            q = jnp.dot(x, w, preferred_element_type=F32).reshape(2, ROWS, WIDE)
            xf = x.astype(F32)
            sq = (xf[:, :HEAD] * xf[:, :HEAD] + xf[:, HEAD:] * xf[:, HEAD:]).reshape(2, ROWS, HEAD)
            ass[...] += sq
            for h in range(2):
                aq[h] += q[:, :, h * HEAD : (h + 1) * HEAD]
                akv[h, :, :, :PIECE] += dot_nt(x, wkv[layer, b, h]).reshape(2, ROWS, PIECE)
            return carry

        lax.fori_loop(0, count, body, 0)

    def heads(layer, beside_step):
        for k in (1 - x_hi, x_hi):
            squares = jnp.sum(ass[k], axis=1, keepdims=True)
            pack(near_s.at[layer, k], aq[1 - c, k], akv[1 - c, k], squares)
            send(near_s.at[layer, k], near_r.at[layer, k], near_ss.at[layer, k], near_rs.at[layer, k], mate)
        beside_step(2)

        def chip_sum(k):
            landed(near_r.at[layer, k], near_ss.at[layer, k], near_rs.at[layer, k])
            squares = jnp.sum(ass[k], axis=1, keepdims=True)
            other = near_r[layer, k].astype(F32)
            tail = jnp.where(lane_at < PIECE, akv[c, k], jnp.where(lane_at == PIECE, squares, 0.0))
            return aq[c, k] + other[:, :HEAD], tail + other[:, HEAD:]

        q, tail = chip_sum(1 - x_hi)
        pack(far_s.at[layer], q, tail, squares_of(tail))
        send(far_s.at[layer], far_r.at[layer], far_ss.at[layer], far_rs.at[layer], across)
        beside_step(3)
        q, tail = chip_sum(x_hi)
        landed(far_r.at[layer], far_ss.at[layer], far_rs.at[layer])
        other = far_r[layer].astype(F32)
        q = q + other[:, :HEAD]
        tail = tail + other[:, HEAD:]
        scale = lax.rsqrt(squares_of(tail) * (1.0 / model) + 1e-06)
        q = (q * scale * HEAD**-0.5).astype(BF16)
        tail_pad[:ROWS, :] = jnp.where(lane_at < PIECE, tail * scale, 0.0).astype(BF16)
        kvs[layer, piece] = dot_nt(select, tail_pad[...]).astype(BF16)
        for n, peer in enumerate(sharers):
            ref = kvs.at[layer, piece]
            send(ref, ref, kv_ss.at[layer, n], kv_rs.at[layer, piece], peer)
        beside_step(4)
        for o in range(1, GROUP):
            p = (piece + o) % GROUP
            landed(kvs.at[layer, p], kv_ss.at[layer, 0], kv_rs.at[layer, p])
        keys = kvs[layer, 0:4].reshape(HEAD, WIDE)
        values = kvs[layer, 4:8].reshape(HEAD, WIDE)
        scores = jnp.dot(q, keys, preferred_element_type=F32)
        scores = jnp.where(mask[...] > 0.5, scores, -1e30)
        top = jnp.max(scores, axis=1, keepdims=True)
        weights = jnp.exp(scores - top)
        probs = (weights / jnp.sum(weights, axis=1, keepdims=True)).astype(BF16)
        place = 2 * x_lo + c
        ctx[layer, x_hi, place] = dot_nt(probs, values).astype(BF16)
        peers = (across, across_beside, across_beside_mate, beside, beside_mate, mate)
        spread(layer, x_hi, peers, 0)
        beside_step(5)

    def spread(layer, k, peers, first):
        ref = ctx.at[layer, k, 2 * x_lo + c]
        for n, peer in enumerate(peers):
            send(ref, ref, ctx_ss.at[layer, first + n], ctx_rs.at[layer, k, 2 * x_lo + c], peer)

    def spread_in(layer, k, place):
        landed(ctx.at[layer, k, place], ctx_ss.at[layer, 0], ctx_rs.at[layer, k, place])

    def reduce(layer, beside_step):
        ks = (x_hi, 1 - x_hi)
        others = (2 * x_lo + 1 - c, 2 * (1 - x_lo) + c, 2 * (1 - x_lo) + 1 - c)

        def products(k, first, last):
            left = jnp.concatenate([ctx[layer, k, n] for n in range(4)], axis=1)

            def body(j, carry):
                b = (z + 3 + j) % nz
                right = wo[layer, b].reshape(4 * HEAD, HEAD)
                pbuf[b, k] = jnp.dot(left, right, preferred_element_type=F32)
                return carry

            lax.fori_loop(first, last, body, 0)

        def block(way, distance):
            return (z + (distance if way == 0 else nz - distance)) % nz

        def put(lane, way, message, value, peers):
            rs_s[layer, lane, way, message] = value.astype(BF16)
            send(
                rs_s.at[layer, lane, way, message],
                rs_r.at[layer, lane, way, message],
                z_ss.at[layer, lane, way, message],
                z_rs.at[layer, lane, way, message],
                peers[way],
            )

        def got(lane, way, message):
            landed(
                rs_r.at[layer, lane, way, message],
                z_ss.at[layer, lane, way, message],
                z_rs.at[layer, lane, way, message],
            )
            return rs_r[layer, lane, way, message].astype(F32)

        def set_out(lane):
            k = ks[lane]
            products(k, 0, 3)
            put(lane, lane, 0, pbuf[block(lane, 4), k], z_second)
            for way in range(2):
                put(lane, way, 1, pbuf[block(way, 3), k], z_next)
            products(k, 3, nz)
            for way in range(2):
                put(lane, way, 3, pbuf[block(way, 1), k], z_next)

        def pass_on(lane):
            for way in range(2):
                value = pbuf[block(way, 2), ks[lane]] + got(lane, way, 1)
                if way == lane:
                    value = value + got(lane, way, 0)
                put(lane, way, 2, value, z_second)

        beside_step(1)
        for place in others:
            spread_in(layer, x_hi, place)
        spread_in(layer, 1 - x_hi, 2 * x_lo + c)
        spread(layer, 1 - x_hi, (mate,), 6)
        set_out(0)
        for place in others:
            spread_in(layer, 1 - x_hi, place)
        set_out(1)
        beside_step(2)
        pass_on(0)
        pass_on(1)
        beside_step(3)

        def collected(lane):
            total = pbuf[z, ks[lane]]
            for way in range(2):
                total = total + got(lane, way, 3) + got(lane, way, 2)
            k = ks[lane]
            if layer == 0:
                old = xs[z, k, :, pl.ds(pl.multiple_of(x_lo * HEAD, HEAD), HEAD)]
            else:
                old = xs_two[z, x_lo, k]
            return (old.astype(F32) + total).astype(BF16)

        return collected

    def nothing(step):
        pass

    clear()
    for b in range(nz):
        loads[("x", b)].wait()
    query_step(0, 2)
    token_forward()
    query_step(0, 3)
    query_step(0, 4)
    output_step(0, 1)
    token_close()
    project(0, y + ny - 3, ny - 1)
    query_step(0, 5)
    project(0, y + 4, 1)
    heads(0, lambda step: output_step(0, step))
    collected = reduce(0, lambda step: query_step(1, step))
    def gather_step(step):
        for lane in range(4):
            k = x_hi if lane < 2 else 1 - x_hi
            half = x_lo if lane % 2 == 0 else 1 - x_lo
            ring_step(
                step,
                lambda b: xs_two.at[b, half, k],
                z,
                nz,
                z_next,
                REACH[(lane // 2 + lane) % 2],
                ag_ss.at[lane],
                ag_rs.at[lane],
                lane % 2 == 0,
            )

    for lane in range(2):
        k = x_hi if lane == 0 else 1 - x_hi
        xs_two[z, x_lo, k] = collected(lane)
        ref = xs_two.at[z, x_lo, k]
        for way in range(2):
            send(ref, ref, ag_ss.at[2 * lane, way, 0], ag_rs.at[2 * lane, way, 0], z_next[way])
        for way in range(2):
            send(ref, ref, ag_ss.at[2 * lane + 1, way, 0], ag_rs.at[2 * lane + 1, way, 0], diagonal[way])
        send(ref, ref, one_ss.at[1 + lane], one_rs.at[1 + k], beside)
    clear()
    gather_step(2)
    query_step(1, 4)
    gather_step(3)
    output_step(1, 1)
    gather_step(4)
    query_step(1, 5)
    for k in range(2):
        landed(xs_two.at[z, 1 - x_lo, k], one_ss.at[1 + k], one_rs.at[1 + k])
    project(1, z + nz - 3, nz - 1)
    gather_step(5)
    project(1, z + 4, 1)
    heads(1, lambda step: output_step(1, step))
    collected = reduce(1, nothing)
    for lane in range(2):
        k = x_hi if lane == 0 else 1 - x_hi
        fin[k] = collected(lane)
    own_half = pl.ds(pl.multiple_of(x_lo * HEAD, HEAD), HEAD)
    moves = [
        copy(fin.at[k], out.at[:, own_half], fin_ss.at[k], fin_rs.at[x_lo], goals[k]) for k in range(2)
    ]
    moves[1].start()

    @pl.when(stays == 0)
    def _():
        moves[0].start()
        moves[0].wait_send()

    @pl.when(stays == 1)
    def _():
        keep = pltpu.make_async_copy(fin.at[0], out.at[:, own_half], local_sem.at[0])
        keep.start()
        keep.wait()

    moves[1].wait_send()
    for move in sent:
        move.wait_send()
    landed(out.at[:, :HEAD], fin_ss.at[0], fin_rs.at[0])

    @pl.when(stays == 0)
    def _():
        landed(out.at[:, HEAD:], fin_ss.at[1], fin_rs.at[1])


def solution(mesh):
    ny, nz = mesh.shape["inst"] // 2, mesh.shape["tp"] // 4

    def shards(tokens, docs, q1, kv1, o1, q2, kv2, o2):
        operands = [pltpu.with_memory_space_constraint(a, pltpu.HBM) for a in (tokens, docs, q1, kv1.T, o1, q2, kv2.T, o2)]
        dma = pltpu.SemaphoreType.DMA
        anywhere = pl.BlockSpec(memory_space=pltpu.HBM)
        vmem = pltpu.VMEM
        return pl.pallas_call(
            functools.partial(kernel, ny, nz),
            out_shape=jax.ShapeDtypeStruct((ROWS, WIDE), BF16),
            in_specs=[anywhere] * 8,
            out_specs=anywhere,
            scratch_shapes=[
                vmem((2, ny, 2, WIDE, HEAD), BF16),
                vmem((2, ny, 2, PIECE, WIDE), BF16),
                vmem((2, ny, 2, 2, HEAD, HEAD), BF16),
                vmem((2 * ny, ROWS), jnp.int32),
                vmem((ROWS, WIDE), F32),
                vmem((nz, 2, ROWS, WIDE), BF16),
                vmem((nz, 2, 2, ROWS, HEAD), BF16),
                vmem((2, 2, ROWS, HEAD), F32),
                vmem((2, 2, ROWS, HEAD), F32),
                vmem((2, ROWS, HEAD), F32),
                vmem((2, 2, ROWS, WIDE), BF16),
                vmem((2, 2, ROWS, WIDE), BF16),
                vmem((2, ROWS, WIDE), BF16),
                vmem((2, ROWS, WIDE), BF16),
                vmem((WIDE, HEAD), BF16),
                vmem((2, GROUP, PIECE, WIDE), BF16),
                vmem((2, 2, 4, ROWS, HEAD), BF16),
                vmem((nz, 2, ROWS, HEAD), F32),
                vmem((2, 2, 2, 4, ROWS, HEAD), BF16),
                vmem((2, 2, 2, 4, ROWS, HEAD), BF16),
                vmem((2, ROWS, HEAD), BF16),
                dma((7,)),
                dma((nz,)),
                dma((2, 5)),
                dma((2, 5)),
                dma((18, 2, 4)),
                dma((18, 2, 4)),
                dma((2, 2, 4)),
                dma((2, 2, 4)),
                dma((2, 2)),
                dma((2, 2)),
                dma((2,)),
                dma((2,)),
                dma((2, GROUP)),
                dma((2, GROUP)),
                dma((2, 7)),
                dma((2, 2, 4)),
                dma((2, 2, 2, 4)),
                dma((2, 2, 2, 4)),
                dma((4, 2, 4)),
                dma((4, 2, 4)),
                dma((4,)),
                dma((4,)),
                dma((2,)),
                dma((2,)),
            ],
            compiler_params=pltpu.CompilerParams(
                collective_id=0,
                has_side_effects=True,
                vmem_limit_bytes=40 * 1024 * 1024,
            ),
            cost_estimate=pl.CostEstimate(
                flops=2_000_000_000, bytes_accessed=10_000_000, transcendentals=51200
            ),
        )(*operands)

    placed = (
        P("inst", None),
        P(),
        P("inst", "tp"),
        P("inst", "tp"),
        P("tp", "inst"),
        P("inst", "tp"),
        P("inst", "tp"),
        P("tp", "inst"),
    )
    return jax.shard_map(
        shards, mesh=mesh, in_specs=placed, out_specs=P("inst", "tp"), check_vma=False
    )
```

```python
import functools

import jax
import jax.numpy as jnp
from jax import lax
from jax.experimental import pallas as pl
from jax.experimental.pallas import tpu as pltpu
from jax.sharding import PartitionSpec as P

MESH = pl.DeviceIdType.MESH
F32 = jnp.float32
BF16 = jnp.bfloat16
NT = (((1,), (1,)), ((), ()))
ROWS = 160
HEAD = 128
PIECE = 32
WIDE = 256
GROUP = 8
REACH = ((4, 3), (3, 4))


def dot_nt(left, right):
    return lax.dot_general(left, right, NT, preferred_element_type=F32)


def kernel(
    ny,
    nz,
    tokens,
    docs,
    query_one,
    keyval_one,
    output_one,
    query_two,
    keyval_two,
    output_two,
    out,
    wq,
    wkv,
    wo,
    docs_in,
    mask,
    xs,
    xs_two,
    aq,
    akv,
    ass,
    near_s,
    near_r,
    far_s,
    far_r,
    tail_pad,
    kvs,
    ctx,
    pbuf,
    rs_s,
    rs_r,
    fin,
    local_sem,
    xlocal_sem,
    swap_ss,
    swap_rs,
    y_ss,
    y_rs,
    far_tok_ss,
    far_tok_rs,
    tok_ss,
    tok_rs,
    near_ss,
    near_rs,
    far_ss,
    far_rs,
    kv_ss,
    kv_rs,
    ctx_ss,
    ctx_rs,
    z_ss,
    z_rs,
    ag_ss,
    ag_rs,
    one_ss,
    one_rs,
    fin_ss,
    fin_rs,
):
    inst = lax.axis_index("inst")
    rank = lax.axis_index("tp")
    ninst, nrank = 2 * ny, 4 * nz
    y, x_hi = inst // 2, inst % 2
    z, x_lo, c = rank // 4, rank // 2 % 2, rank % 2
    piece = rank % GROUP
    model = ny * 2 * 512

    mate = (inst, rank + 1 - 2 * c)
    across = (inst + 1 - 2 * x_hi, rank)
    beside = (inst, rank + 2 - 4 * x_lo)
    y_next = (((inst + 2) % ninst, rank), ((inst + ninst - 2) % ninst, rank))
    y_next_mate = tuple((peer, rank + 1 - 2 * c) for peer, _ in y_next)
    z_next = ((inst, (rank + 4) % nrank), (inst, (rank + nrank - 4) % nrank))
    across_beside = (inst + 1 - 2 * x_hi, rank + 2 - 4 * x_lo)
    across_beside_mate = (inst + 1 - 2 * x_hi, rank + 3 - 4 * x_lo - 2 * c)
    beside_mate = (inst, rank + 3 - 4 * x_lo - 2 * c)
    goals = [((2 * y + k + 1) % ninst, 4 * z + 2 * x_hi + c) for k in range(2)]
    origin_inst = (inst + ninst - 1) % ninst // 2 * 2 + x_lo
    origins = [(origin_inst, 4 * z + 2 * s + c) for s in range(2)]
    stays = x_hi * x_lo

    group_base = rank // GROUP * GROUP
    sharers = [(inst, group_base + (piece + o) % GROUP) for o in range(1, GROUP)]
    other_rank = (rank + nrank + 4 * (2 * (z % 2) - 1)) % nrank
    other_z = (inst, other_rank)
    other_diagonal = (inst, other_rank + 2 - 4 * x_lo)
    z_second = ((inst, (rank + 8) % nrank), (inst, (rank + nrank - 8) % nrank))
    diagonal = tuple((inst, peer + 2 - 4 * x_lo) for _, peer in z_next)

    barrier = pltpu.get_barrier_semaphore()
    greeted = sharers + [other_z, other_diagonal, *z_second, *y_next, across, origins[0]]
    greeted += [across_beside, across_beside_mate, *y_next_mate]
    for peer in greeted:
        pl.semaphore_signal(barrier, inc=1, device_id=peer, device_id_type=MESH)

    @pl.when(stays == 0)
    def _():
        pl.semaphore_signal(barrier, inc=1, device_id=origins[1], device_id_type=MESH)

    sent = []

    def copy(src, dst, send, recv, peer):
        return pltpu.make_async_remote_copy(
            src_ref=src,
            dst_ref=dst,
            send_sem=send,
            recv_sem=recv,
            device_id=peer,
            device_id_type=MESH,
        )

    def send(*args):
        move = copy(*args)
        move.start()
        sent.append(move)

    def drain(kept):
        while len(sent) > kept:
            sent.pop(0).wait_send()

    def landed(dst, send_sem, recv_sem):
        copy(dst, dst, send_sem, recv_sem, mate).wait_recv()

    queries = (query_one, query_two)
    keyvals = (keyval_one, keyval_two)
    outputs = (output_one, output_two)
    loads = {}

    def load(name, src, dst, sem):
        loads[name] = pltpu.make_async_copy(src, dst, sem)
        loads[name].start()

    def quarter(block, hi):
        return pl.ds(pl.multiple_of((2 * block + hi) * 512 + c * WIDE, WIDE), WIDE)

    own_k = pl.ds(pl.multiple_of(c * WIDE, WIDE), WIDE)
    mate_k = pl.ds(pl.multiple_of((1 - c) * WIDE, WIDE), WIDE)
    own_part = pl.ds(pl.multiple_of((2 * c + x_lo) * HEAD, HEAD), HEAD)
    load("kv0", keyvals[0].at[:, own_k], wkv.at[0, y, c], local_sem.at[0])
    load("q0", queries[0].at[own_k, :], wq.at[0, y, c], local_sem.at[1])
    for b in range(nz):
        load(("x", b), tokens.at[:, quarter(b, x_hi)], xs.at[b, x_hi], xlocal_sem.at[b])
    load("o0", outputs[0].at[:, own_part], wo.at[0, y, x_lo, c], local_sem.at[2])
    load("docs", docs, docs_in, local_sem.at[3])
    load("kv1", keyvals[1].at[:, own_k], wkv.at[1, y, c], local_sem.at[4])
    load("q1", queries[1].at[own_k, :], wq.at[1, y, c], local_sem.at[5])
    load("o1", outputs[1].at[:, own_part], wo.at[1, y, x_lo, c], local_sem.at[6])

    pl.semaphore_wait(barrier, len(greeted) + 1 - stays)

    def swap(layer, n, src, dst, peer):
        send(src, dst, swap_ss.at[layer, n], swap_rs.at[layer, n], peer)

    def swapped(layer, n, dst):
        landed(dst, swap_ss.at[layer, n], swap_rs.at[layer, n])

    def swap_query(layer):
        swap(layer, 0, queries[layer].at[mate_k, :], wq.at[layer, y, c], mate)
        swap(layer, 1, keyvals[layer].at[:, mate_k], wkv.at[layer, y, c], mate)

    def part(lo, core):
        return pl.ds(pl.multiple_of((2 * core + lo) * HEAD, HEAD), HEAD)

    def swap_output(layer):
        dst = wo.at[layer, y, x_lo, c]
        swap(layer, 2, outputs[layer].at[:, part(x_lo, 1 - c)], dst, mate)
        swap(layer, 3, outputs[layer].at[:, part(1 - x_lo, c)], dst, beside)
        swap(layer, 4, outputs[layer].at[:, part(1 - x_lo, 1 - c)], dst, beside_mate)

    def ring_step(step, lanes, me, n, peers):
        for slot, reach, ss, rs, opens in lanes:
            for way in range(2):
                block = (me + (n - 1 if way == 0 else 1) * (step - 1)) % n
                if 1 < step <= reach[way] + 1:
                    landed(slot(block), ss.at[way, step - 2], rs.at[way, step - 2])
                if step <= reach[way] and (opens or step > 1):
                    ref = slot(block)
                    send(ref, ref, ss.at[way, step - 1], rs.at[way, step - 1], peers[way])

    def query_open(layer):
        for way in range(2):
            for keep in range(2):
                core = c if keep == 0 else 1 - c
                peer = y_next[way] if keep == 0 else y_next_mate[way]
                for part in range(2):
                    unit = 10 * layer + 2 * keep + part
                    rows = pl.ds(pl.multiple_of(core * WIDE + part * HEAD, HEAD), HEAD)
                    dst = wq.at[layer, y, c, pl.ds(part * HEAD, HEAD)]
                    send(queries[layer].at[rows, :], dst, y_ss.at[unit, way, 0], y_rs.at[unit, way, 0], peer)
                unit = 10 * layer + 4 + keep
                src = keyvals[layer].at[:, own_k if keep == 0 else mate_k]
                send(src, wkv.at[layer, y, c], y_ss.at[unit, way, 0], y_rs.at[unit, way, 0], peer)

    def query_step(layer, step):
        def lane_of(lane):
            keep = lane // 2 if lane < 4 else lane - 4
            head = c if keep == 0 else 1 - c
            rows = pl.ds(lane % 2 * HEAD, HEAD)

            def slot(b):
                return wq.at[layer, b, head, rows] if lane < 4 else wkv.at[layer, b, head]

            unit = 10 * layer + lane
            return slot, REACH[lane % 2], y_ss.at[unit], y_rs.at[unit], False

        ring_step(step, [lane_of(lane) for lane in range(6)], y, ny, y_next)

    def query_ready(layer):
        loads[f"q{layer}"].wait()
        loads[f"kv{layer}"].wait()
        swapped(layer, 0, wq.at[layer, y, 1 - c])
        swapped(layer, 1, wkv.at[layer, y, 1 - c])

    def output_step(layer, step):
        def lane_of(lane):
            lo = x_lo if lane < 2 else 1 - x_lo
            core = c if lane % 2 == 0 else 1 - c
            unit = 10 * layer + 6 + lane
            return lambda b: wo.at[layer, b, lo, core], REACH[lane % 2], y_ss.at[unit], y_rs.at[unit], True

        if step == 1:
            loads[f"o{layer}"].wait()
            for lane in range(1, 4):
                lo = x_lo if lane < 2 else 1 - x_lo
                swapped(layer, 1 + lane, wo.at[layer, y, lo, c if lane % 2 == 0 else 1 - c])
        ring_step(step, [lane_of(lane) for lane in range(4)], y, ny, y_next)

    def token_block(offset):
        return xs.at[(z + offset) % nz, 1 - x_hi]

    def token_open():
        for n, offset in enumerate((0, 2, 6, 4)):
            b = (z + offset) % nz
            src = tokens.at[:, quarter(b, 1 - x_hi)]
            send(src, xs.at[b, x_hi], far_tok_ss.at[n], far_tok_rs.at[n], across_beside)

    def token_forward(n, offset, ways):
        ref = token_block(offset)
        landed(ref, far_tok_ss.at[n], far_tok_rs.at[n])
        for way in ways:
            place = 0 if n == 0 else 1
            send(ref, ref, tok_ss.at[way, place], tok_rs.at[way, place], z_next[way])

    def token_close():
        token_forward(3, 4, ())
        for way, first, second in ((0, 7, 5), (1, 1, 3)):
            landed(token_block(first), tok_ss.at[way, 0], tok_rs.at[way, 0])
            landed(token_block(second), tok_ss.at[way, 1], tok_rs.at[way, 1])

    query_open(0)
    token_open()
    swap_query(0)
    swap_output(0)

    loads["docs"].wait()
    doc_row = jnp.broadcast_to(docs_in[pl.ds(inst, 1), :], (ROWS, ROWS)).astype(F32)
    place_t = lax.broadcasted_iota(jnp.int32, (ROWS, ROWS), 0)
    place_s = lax.broadcasted_iota(jnp.int32, (ROWS, ROWS), 1)
    doc_col = dot_nt((place_t == place_s).astype(BF16), doc_row.astype(BF16))
    allowed = (doc_col == doc_row) & (place_s <= place_t)
    mask[...] = jnp.zeros_like(mask)
    mask[:, :ROWS] = jnp.where(allowed, 1.0, 0.0)
    tail_pad[...] = jnp.zeros_like(tail_pad)

    lane_at = lax.broadcasted_iota(jnp.int32, (ROWS, HEAD), 1)
    select = (
        lax.broadcasted_iota(jnp.int32, (PIECE, HEAD), 0)
        == lax.broadcasted_iota(jnp.int32, (PIECE, HEAD), 1)
    ).astype(BF16)

    def pack(ref, q, tail, squares):
        high = squares.astype(BF16).astype(F32)
        low = squares - high
        tail = jnp.where(lane_at < PIECE, tail, jnp.where(lane_at == PIECE, high, 0.0))
        tail = jnp.where(lane_at == PIECE + 1, low, tail)
        ref[:, :HEAD] = q.astype(BF16)
        ref[:, HEAD:] = tail.astype(BF16)

    def squares_of(tail):
        return jnp.sum(jnp.where(lane_at < PIECE, 0.0, tail), axis=1, keepdims=True)

    def clear():
        aq[...] = jnp.zeros_like(aq)
        akv[...] = jnp.zeros_like(akv)
        ass[...] = jnp.zeros_like(ass)

    def project(layer, first, count):
        def body(j, carry):
            b = (first + j) % nz
            if layer == 0:
                x = xs[b].reshape(2 * ROWS, WIDE)
            else:
                x = jnp.concatenate([xs_two[b, 0].reshape(2 * ROWS, HEAD), xs_two[b, 1].reshape(2 * ROWS, HEAD)], axis=1)
            w = jnp.concatenate([wq[layer, b, 0], wq[layer, b, 1]], axis=1)
            q = jnp.dot(x, w, preferred_element_type=F32).reshape(2, ROWS, WIDE)
            xf = x.astype(F32)
            sq = (xf[:, :HEAD] * xf[:, :HEAD] + xf[:, HEAD:] * xf[:, HEAD:]).reshape(2, ROWS, HEAD)
            ass[...] += sq
            for h in range(2):
                aq[h] += q[:, :, h * HEAD : (h + 1) * HEAD]
                akv[h, :, :, :PIECE] += dot_nt(x, wkv[layer, b, h]).reshape(2, ROWS, PIECE)
            return carry

        lax.fori_loop(0, count, body, 0)

    def heads(layer, beside_step):
        for k in (1 - x_hi, x_hi):
            squares = jnp.sum(ass[k], axis=1, keepdims=True)
            pack(near_s.at[layer, k], aq[1 - c, k], akv[1 - c, k], squares)
            send(near_s.at[layer, k], near_r.at[layer, k], near_ss.at[layer, k], near_rs.at[layer, k], mate)
        beside_step(2)

        def chip_sum(k):
            landed(near_r.at[layer, k], near_ss.at[layer, k], near_rs.at[layer, k])
            squares = jnp.sum(ass[k], axis=1, keepdims=True)
            other = near_r[layer, k].astype(F32)
            tail = jnp.where(lane_at < PIECE, akv[c, k], jnp.where(lane_at == PIECE, squares, 0.0))
            return aq[c, k] + other[:, :HEAD], tail + other[:, HEAD:]

        q, tail = chip_sum(1 - x_hi)
        pack(far_s.at[layer], q, tail, squares_of(tail))
        send(far_s.at[layer], far_r.at[layer], far_ss.at[layer], far_rs.at[layer], across)
        beside_step(3)
        q, tail = chip_sum(x_hi)
        landed(far_r.at[layer], far_ss.at[layer], far_rs.at[layer])
        other = far_r[layer].astype(F32)
        q = q + other[:, :HEAD]
        tail = tail + other[:, HEAD:]
        scale = lax.rsqrt(squares_of(tail) * (1.0 / model) + 1e-06)
        q = (q * scale * HEAD**-0.5).astype(BF16)
        tail_pad[:ROWS, :] = jnp.where(lane_at < PIECE, tail * scale, 0.0).astype(BF16)
        kvs[layer, piece] = dot_nt(select, tail_pad[...]).astype(BF16)
        for n, peer in enumerate(sharers):
            ref = kvs.at[layer, piece]
            send(ref, ref, kv_ss.at[layer, n], kv_rs.at[layer, piece], peer)
        beside_step(4)
        drain(20)
        for o in range(1, GROUP):
            p = (piece + o) % GROUP
            landed(kvs.at[layer, p], kv_ss.at[layer, 0], kv_rs.at[layer, p])
        keys = kvs[layer, 0:4].reshape(HEAD, WIDE)
        values = kvs[layer, 4:8].reshape(HEAD, WIDE)
        scores = jnp.dot(q, keys, preferred_element_type=F32)
        scores = jnp.where(mask[...] > 0.5, scores, -1e30)
        top = jnp.max(scores, axis=1, keepdims=True)
        weights = jnp.exp(scores - top)
        probs = (weights / jnp.sum(weights, axis=1, keepdims=True)).astype(BF16)
        place = 2 * x_lo + c
        ctx[layer, x_hi, place] = dot_nt(probs, values).astype(BF16)
        peers = (beside, beside_mate, across, mate, across_beside, across_beside_mate)
        spread(layer, x_hi, peers, 0)
        beside_step(5)

    def spread(layer, k, peers, first):
        ref = ctx.at[layer, k, 2 * x_lo + c]
        for n, peer in enumerate(peers):
            send(ref, ref, ctx_ss.at[layer, first + n], ctx_rs.at[layer, k, 2 * x_lo + c], peer)

    def spread_in(layer, k, place):
        landed(ctx.at[layer, k, place], ctx_ss.at[layer, 0], ctx_rs.at[layer, k, place])

    def reduce(layer, beside_step):
        ks = (x_hi, 1 - x_hi)
        others = (2 * x_lo + 1 - c, 2 * (1 - x_lo) + c, 2 * (1 - x_lo) + 1 - c)

        def products(k, first, last):
            left = jnp.concatenate([ctx[layer, k, n] for n in range(4)], axis=1)

            def body(j, carry):
                b, b_next = (z + 3 + 2 * j) % nz, (z + 4 + 2 * j) % nz
                right = jnp.concatenate(
                    [wo[layer, b].reshape(4 * HEAD, HEAD), wo[layer, b_next].reshape(4 * HEAD, HEAD)], axis=1
                )
                both = jnp.dot(left, right, preferred_element_type=F32)
                pbuf[b, k] = both[:, :HEAD]
                pbuf[b_next, k] = both[:, HEAD:]
                return carry

            lax.fori_loop(first, last, body, 0)

        def block(way, distance):
            return (z + (distance if way == 0 else nz - distance)) % nz

        def put(lane, way, message, value, peers):
            rs_s[layer, lane, way, message] = value.astype(BF16)
            send(
                rs_s.at[layer, lane, way, message],
                rs_r.at[layer, lane, way, message],
                z_ss.at[layer, lane, way, message],
                z_rs.at[layer, lane, way, message],
                peers[way],
            )

        def got(lane, way, message):
            landed(
                rs_r.at[layer, lane, way, message],
                z_ss.at[layer, lane, way, message],
                z_rs.at[layer, lane, way, message],
            )
            return rs_r[layer, lane, way, message].astype(F32)

        def set_out(lane):
            k = ks[lane]
            products(k, 0, 2)
            put(lane, lane, 0, pbuf[block(lane, 4), k], z_second)
            for way in range(2):
                put(lane, way, 1, pbuf[block(way, 3), k], z_next)
            products(k, 2, nz // 2)
            for way in range(2):
                put(lane, way, 3, pbuf[block(way, 1), k], z_next)

        def pass_on(lane):
            for way in range(2):
                value = pbuf[block(way, 2), ks[lane]] + got(lane, way, 1)
                if way == lane:
                    value = value + got(lane, way, 0)
                put(lane, way, 2, value, z_second)

        beside_step(1)
        for place in others:
            spread_in(layer, x_hi, place)
        output_step(layer, 5)
        set_out(0)
        spread_in(layer, 1 - x_hi, 2 * x_lo + c)
        spread(layer, 1 - x_hi, (mate,), 6)
        for place in others:
            spread_in(layer, 1 - x_hi, place)
        set_out(1)
        beside_step(2)
        drain(20)
        pass_on(0)
        pass_on(1)
        beside_step(3)

        def collected(lane):
            total = pbuf[z, ks[lane]]
            for way in range(2):
                total = total + got(lane, way, 3) + got(lane, way, 2)
            k = ks[lane]
            if layer == 0:
                old = xs[z, k, :, pl.ds(pl.multiple_of(x_lo * HEAD, HEAD), HEAD)]
            else:
                old = xs_two[z, x_lo, k]
            return (old.astype(F32) + total).astype(BF16)

        return collected

    def nothing(step):
        pass

    clear()
    for b in range(nz):
        loads[("x", b)].wait()
    query_step(0, 2)
    token_forward(0, 0, (0, 1))
    swap_query(1)
    swap_output(1)
    token_forward(1, 2, (1,))
    query_step(0, 3)
    token_forward(2, 6, (0,))
    output_step(0, 1)
    query_step(0, 4)
    query_ready(0)
    token_close()
    project(0, y + ny - 3, ny - 1)
    output_step(0, 2)
    query_step(0, 5)
    project(0, y + 4, 1)
    def beside_heads(step):
        if step in (3, 4):
            output_step(0, step)

    heads(0, beside_heads)
    collected = reduce(0, lambda step: query_open(1) if step == 1 else query_step(1, step))
    def gather_step(step):
        def lane_of(lane):
            k = x_hi if lane < 2 else 1 - x_hi
            half = x_lo if lane % 2 == 0 else 1 - x_lo
            reach = REACH[(lane // 2 + lane) % 2]
            return lambda b: xs_two.at[b, half, k], reach, ag_ss.at[lane], ag_rs.at[lane], lane % 2 == 0

        ring_step(step, [lane_of(lane) for lane in range(4)], z, nz, z_next)

    for lane in range(2):
        k = x_hi if lane == 0 else 1 - x_hi
        xs_two[z, x_lo, k] = collected(lane)
        ref = xs_two.at[z, x_lo, k]
        for way in range(2):
            send(ref, ref, ag_ss.at[2 * lane, way, 0], ag_rs.at[2 * lane, way, 0], z_next[way])
        for way in range(2):
            send(ref, ref, ag_ss.at[2 * lane + 1, way, 0], ag_rs.at[2 * lane + 1, way, 0], diagonal[way])
        send(ref, ref, one_ss.at[1 + lane], one_rs.at[1 + k], beside)
    clear()
    gather_step(2)
    query_step(1, 4)
    gather_step(3)
    gather_step(4)
    query_step(1, 5)
    for k in range(2):
        landed(xs_two.at[z, 1 - x_lo, k], one_ss.at[1 + k], one_rs.at[1 + k])
    query_ready(1)
    project(1, z + nz - 3, nz - 1)
    gather_step(5)
    project(1, z + 4, 1)
    heads(1, lambda step: output_step(1, step - 1))
    collected = reduce(1, nothing)
    for lane in range(2):
        k = x_hi if lane == 0 else 1 - x_hi
        fin[k] = collected(lane)
    own_half = pl.ds(pl.multiple_of(x_lo * HEAD, HEAD), HEAD)
    moves = [
        copy(fin.at[k], out.at[:, own_half], fin_ss.at[k], fin_rs.at[x_lo], goals[k]) for k in range(2)
    ]
    moves[1].start()

    @pl.when(stays == 0)
    def _():
        moves[0].start()
        moves[0].wait_send()

    @pl.when(stays == 1)
    def _():
        keep = pltpu.make_async_copy(fin.at[0], out.at[:, own_half], local_sem.at[0])
        keep.start()
        keep.wait()

    moves[1].wait_send()
    drain(0)
    landed(out.at[:, :HEAD], fin_ss.at[0], fin_rs.at[0])

    @pl.when(stays == 0)
    def _():
        landed(out.at[:, HEAD:], fin_ss.at[1], fin_rs.at[1])


def solution(mesh):
    ny, nz = mesh.shape["inst"] // 2, mesh.shape["tp"] // 4

    def shards(tokens, docs, q1, kv1, o1, q2, kv2, o2):
        operands = [pltpu.with_memory_space_constraint(a, pltpu.HBM) for a in (tokens, docs, q1, kv1.T, o1, q2, kv2.T, o2)]
        dma = pltpu.SemaphoreType.DMA
        anywhere = pl.BlockSpec(memory_space=pltpu.HBM)
        vmem = pltpu.VMEM
        return pl.pallas_call(
            functools.partial(kernel, ny, nz),
            out_shape=jax.ShapeDtypeStruct((ROWS, WIDE), BF16),
            in_specs=[anywhere] * 8,
            out_specs=anywhere,
            scratch_shapes=[
                vmem((2, ny, 2, WIDE, HEAD), BF16),
                vmem((2, ny, 2, PIECE, WIDE), BF16),
                vmem((2, ny, 2, 2, HEAD, HEAD), BF16),
                vmem((2 * ny, ROWS), jnp.int32),
                vmem((ROWS, WIDE), F32),
                vmem((nz, 2, ROWS, WIDE), BF16),
                vmem((nz, 2, 2, ROWS, HEAD), BF16),
                vmem((2, 2, ROWS, HEAD), F32),
                vmem((2, 2, ROWS, HEAD), F32),
                vmem((2, ROWS, HEAD), F32),
                vmem((2, 2, ROWS, WIDE), BF16),
                vmem((2, 2, ROWS, WIDE), BF16),
                vmem((2, ROWS, WIDE), BF16),
                vmem((2, ROWS, WIDE), BF16),
                vmem((WIDE, HEAD), BF16),
                vmem((2, GROUP, PIECE, WIDE), BF16),
                vmem((2, 2, 4, ROWS, HEAD), BF16),
                vmem((nz, 2, ROWS, HEAD), F32),
                vmem((2, 2, 2, 4, ROWS, HEAD), BF16),
                vmem((2, 2, 2, 4, ROWS, HEAD), BF16),
                vmem((2, ROWS, HEAD), BF16),
                dma((7,)),
                dma((nz,)),
                dma((2, 5)),
                dma((2, 5)),
                dma((20, 2, 4)),
                dma((20, 2, 4)),
                dma((4,)),
                dma((4,)),
                dma((2, 2)),
                dma((2, 2)),
                dma((2, 2)),
                dma((2, 2)),
                dma((2,)),
                dma((2,)),
                dma((2, GROUP)),
                dma((2, GROUP)),
                dma((2, 7)),
                dma((2, 2, 4)),
                dma((2, 2, 2, 4)),
                dma((2, 2, 2, 4)),
                dma((4, 2, 4)),
                dma((4, 2, 4)),
                dma((4,)),
                dma((4,)),
                dma((2,)),
                dma((2,)),
            ],
            compiler_params=pltpu.CompilerParams(
                collective_id=0,
                has_side_effects=True,
                vmem_limit_bytes=40 * 1024 * 1024,
            ),
            cost_estimate=pl.CostEstimate(
                flops=2_000_000_000, bytes_accessed=10_000_000, transcendentals=51200
            ),
        )(*operands)

    placed = (
        P("inst", None),
        P(),
        P("inst", "tp"),
        P("inst", "tp"),
        P("tp", "inst"),
        P("inst", "tp"),
        P("inst", "tp"),
        P("tp", "inst"),
    )
    return jax.shard_map(
        shards, mesh=mesh, in_specs=placed, out_specs=P("inst", "tp"), check_vma=False
    )
```

```python
import functools

import jax
import jax.numpy as jnp
from jax import lax
from jax.experimental import pallas as pl
from jax.experimental.pallas import tpu as pltpu
from jax.sharding import PartitionSpec as P

MESH = pl.DeviceIdType.MESH
F32 = jnp.float32
BF16 = jnp.bfloat16
NT = (((1,), (1,)), ((), ()))
ROWS = 160
HEAD = 128
PIECE = 32
WIDE = 256
GROUP = 8
REACH = ((4, 3), (3, 4))


def dot_nt(left, right):
    return lax.dot_general(left, right, NT, preferred_element_type=F32)


def kernel(
    ny,
    nz,
    tokens,
    docs,
    query_one,
    keyval_one,
    output_one,
    query_two,
    keyval_two,
    output_two,
    out,
    wq,
    wkv,
    wo,
    docs_in,
    mask,
    xs,
    xs_own,
    xs_two,
    aq,
    akv,
    ass,
    near_s,
    near_r,
    far_s,
    far_r,
    tail_pad,
    kvs,
    ctx,
    pbuf,
    rs_s,
    rs_r,
    fin,
    local_sem,
    own_sem,
    xlocal_sem,
    swap_ss,
    swap_rs,
    y_ss,
    y_rs,
    far_tok_ss,
    far_tok_rs,
    mate_tok_ss,
    mate_tok_rs,
    tok_ss,
    tok_rs,
    near_ss,
    near_rs,
    far_ss,
    far_rs,
    kv_ss,
    kv_rs,
    ctx_ss,
    ctx_rs,
    z_ss,
    z_rs,
    ag_ss,
    ag_rs,
    one_ss,
    one_rs,
    fin_ss,
    fin_rs,
):
    inst = lax.axis_index("inst")
    rank = lax.axis_index("tp")
    ninst, nrank = 2 * ny, 4 * nz
    y, x_hi = inst // 2, inst % 2
    z, x_lo, c = rank // 4, rank // 2 % 2, rank % 2
    piece = rank % GROUP
    model = ny * 2 * 512

    mate = (inst, rank + 1 - 2 * c)
    across = (inst + 1 - 2 * x_hi, rank)
    beside = (inst, rank + 2 - 4 * x_lo)
    y_next = (((inst + 2) % ninst, rank), ((inst + ninst - 2) % ninst, rank))
    y_next_mate = tuple((peer, rank + 1 - 2 * c) for peer, _ in y_next)
    z_next = ((inst, (rank + 4) % nrank), (inst, (rank + nrank - 4) % nrank))
    across_beside = (inst + 1 - 2 * x_hi, rank + 2 - 4 * x_lo)
    across_beside_mate = (inst + 1 - 2 * x_hi, rank + 3 - 4 * x_lo - 2 * c)
    beside_mate = (inst, rank + 3 - 4 * x_lo - 2 * c)
    origin_inst = (inst + ninst - 1) % ninst // 2 * 2 + x_lo
    origins = [(origin_inst, 4 * z + 2 * s + c) for s in range(2)]
    stays = x_hi * x_lo

    group_base = rank // GROUP * GROUP
    sharers = [(inst, group_base + (piece + o) % GROUP) for o in range(1, GROUP)]
    other_rank = (rank + nrank + 4 * (2 * (z % 2) - 1)) % nrank
    other_z = (inst, other_rank)
    other_diagonal = (inst, other_rank + 2 - 4 * x_lo)
    z_second = ((inst, (rank + 8) % nrank), (inst, (rank + nrank - 8) % nrank))
    diagonal = tuple((inst, peer + 2 - 4 * x_lo) for _, peer in z_next)

    barrier = pltpu.get_barrier_semaphore()
    greeted = [*y_next, across_beside, *y_next_mate, *sharers, other_z, other_diagonal, *z_second]
    greeted += [across, across_beside_mate, origins[0]]
    for peer in greeted:
        pl.semaphore_signal(barrier, inc=1, device_id=peer, device_id_type=MESH)

    @pl.when(stays == 0)
    def _():
        pl.semaphore_signal(barrier, inc=1, device_id=origins[1], device_id_type=MESH)

    sent = []

    def copy(src, dst, send, recv, peer):
        return pltpu.make_async_remote_copy(
            src_ref=src,
            dst_ref=dst,
            send_sem=send,
            recv_sem=recv,
            device_id=peer,
            device_id_type=MESH,
        )

    def send(*args):
        move = copy(*args)
        move.start()
        sent.append(move)

    def drain(kept):
        while len(sent) > kept:
            sent.pop(0).wait_send()

    def landed(dst, send_sem, recv_sem):
        copy(dst, dst, send_sem, recv_sem, mate).wait_recv()

    queries = (query_one, query_two)
    keyvals = (keyval_one, keyval_two)
    outputs = (output_one, output_two)
    loads = {}

    def load(name, src, dst, sem):
        loads[name] = pltpu.make_async_copy(src, dst, sem)
        loads[name].start()

    def quarter(block, hi):
        return pl.ds(pl.multiple_of((2 * block + hi) * 512 + c * WIDE, WIDE), WIDE)

    own_k = pl.ds(pl.multiple_of(c * WIDE, WIDE), WIDE)
    mate_k = pl.ds(pl.multiple_of((1 - c) * WIDE, WIDE), WIDE)
    halves = [pl.ds(half * WIDE, WIDE) for half in range(2)]
    pl.semaphore_wait(barrier, len(greeted) + 1 - stays)

    def swap(layer, n, src, dst, peer):
        send(src, dst, swap_ss.at[layer, n], swap_rs.at[layer, n], peer)

    def swapped(layer, n, dst):
        landed(dst, swap_ss.at[layer, n], swap_rs.at[layer, n])

    def swap_query(layer):
        swap(layer, 0, queries[layer].at[mate_k, :], wq.at[layer, y, c], mate)
        swap(layer, 1, keyvals[layer].at[:, mate_k], wkv.at[layer, y, c], mate)

    def part(lo, core):
        return pl.ds(pl.multiple_of((2 * core + lo) * HEAD, HEAD), HEAD)

    def swap_output(layer):
        dst = wo.at[layer, y, x_lo, c]
        swap(layer, 2, outputs[layer].at[:, part(x_lo, 1 - c)], dst, mate)
        swap(layer, 3, outputs[layer].at[:, part(1 - x_lo, c)], dst, beside)
        swap(layer, 4, outputs[layer].at[:, part(1 - x_lo, 1 - c)], dst, beside_mate)

    def ring_step(step, lanes, me, n, peers):
        for slot, reach, ss, rs, opens in lanes:
            for way in range(2):
                block = (me + (n - 1 if way == 0 else 1) * (step - 1)) % n
                if 1 < step <= reach[way] + 1:
                    landed(slot(block), ss.at[way, step - 2], rs.at[way, step - 2])
                if step <= reach[way] and (opens or step > 1):
                    ref = slot(block)
                    send(ref, ref, ss.at[way, step - 1], rs.at[way, step - 1], peers[way])

    def query_open(layer):
        for way in range(2):
            if layer == 0:
                for half in range(2):
                    for part in range(2):
                        unit = 2 * half + part
                        rows = pl.ds(half * WIDE + part * HEAD, HEAD)
                        dst = wq.at[0, y, half, pl.ds(part * HEAD, HEAD)]
                        send(queries[0].at[rows, :], dst, y_ss.at[unit, way, 0], y_rs.at[unit, way, 0], y_next[way])
                    src = keyvals[0].at[:, halves[half]]
                    unit = 4 + half
                    send(src, wkv.at[0, y, half], y_ss.at[unit, way, 0], y_rs.at[unit, way, 0], y_next[way])
                continue
            for keep in range(2):
                core = c if keep == 0 else 1 - c
                peer = y_next[way] if keep == 0 else y_next_mate[way]
                for part in range(2):
                    unit = 10 * layer + 2 * keep + part
                    rows = pl.ds(pl.multiple_of(core * WIDE + part * HEAD, HEAD), HEAD)
                    dst = wq.at[layer, y, c, pl.ds(part * HEAD, HEAD)]
                    send(queries[layer].at[rows, :], dst, y_ss.at[unit, way, 0], y_rs.at[unit, way, 0], peer)
                unit = 10 * layer + 4 + keep
                src = keyvals[layer].at[:, own_k if keep == 0 else mate_k]
                send(src, wkv.at[layer, y, c], y_ss.at[unit, way, 0], y_rs.at[unit, way, 0], peer)

    def query_step(layer, step):
        def lane_of(lane):
            keep = lane // 2 if lane < 4 else lane - 4
            head = keep if layer == 0 else c if keep == 0 else 1 - c
            rows = pl.ds(lane % 2 * HEAD, HEAD)

            def slot(b):
                return wq.at[layer, b, head, rows] if lane < 4 else wkv.at[layer, b, head]

            unit = 10 * layer + lane
            return slot, REACH[lane % 2], y_ss.at[unit], y_rs.at[unit], False

        ring_step(step, [lane_of(lane) for lane in range(6)], y, ny, y_next)

    def query_ready(layer):
        if layer == 0:
            for half in range(2):
                loads["q0", half].wait()
                loads["kv0", half].wait()
            return
        loads[f"q{layer}"].wait()
        loads[f"kv{layer}"].wait()
        swapped(layer, 0, wq.at[layer, y, 1 - c])
        swapped(layer, 1, wkv.at[layer, y, 1 - c])

    def output_step(layer, step):
        def lane_of(lane):
            lo = x_lo if lane < 2 else 1 - x_lo
            core = c if lane % 2 == 0 else 1 - c
            unit = 10 * layer + 6 + lane
            return lambda b: wo.at[layer, b, lo, core], REACH[lane % 2], y_ss.at[unit], y_rs.at[unit], True

        if step == 1:
            loads[f"o{layer}"].wait()
            for lane in range(1, 4):
                lo = x_lo if lane < 2 else 1 - x_lo
                swapped(layer, 1 + lane, wo.at[layer, y, lo, c if lane % 2 == 0 else 1 - c])
        ring_step(step, [lane_of(lane) for lane in range(4)], y, ny, y_next)

    def token_block(offset):
        return xs.at[(z + offset) % nz, c]

    def token_open():
        for n, offset in enumerate((0, 2, 6, 4)):
            b = (z + offset) % nz
            src = tokens.at[:, quarter(b, 1 - x_hi)]
            send(src, xs.at[b, c], far_tok_ss.at[n], far_tok_rs.at[n], across_beside)

    def token_forward(n, offset, ways):
        ref = token_block(offset)
        landed(ref, far_tok_ss.at[n], far_tok_rs.at[n])
        for way in ways:
            place = 0 if n == 0 else 1
            send(ref, ref, tok_ss.at[way, place], tok_rs.at[way, place], z_next[way])
        token_share(offset)

    def token_share(offset):
        ref = token_block(offset)
        send(ref, ref, mate_tok_ss.at[offset], mate_tok_rs.at[offset], mate)

    def token_close():
        token_forward(3, 4, ())
        for way, first, second in ((0, 7, 5), (1, 1, 3)):
            landed(token_block(first), tok_ss.at[way, 0], tok_rs.at[way, 0])
            token_share(first)
            landed(token_block(second), tok_ss.at[way, 1], tok_rs.at[way, 1])
            token_share(second)

    def token_finish():
        for offset in range(nz):
            landed(xs.at[(z + offset) % nz, 1 - c], mate_tok_ss.at[offset], mate_tok_rs.at[offset])

    query_open(0)
    token_open()
    own_part = pl.ds(pl.multiple_of((2 * c + x_lo) * HEAD, HEAD), HEAD)
    for half in range(2):
        load(("kv0", half), keyvals[0].at[:, halves[half]], wkv.at[0, y, half], own_sem.at[half])
        load(("q0", half), queries[0].at[halves[half], :], wq.at[0, y, half], own_sem.at[2 + half])
    for b in range(nz):
        columns = pl.ds(pl.multiple_of((2 * b + x_hi) * 512, 512), 512)
        load(("x", b), tokens.at[:, columns], xs_own.at[b], xlocal_sem.at[b])
    load("o0", outputs[0].at[:, own_part], wo.at[0, y, x_lo, c], local_sem.at[2])
    load("docs", docs, docs_in, local_sem.at[3])
    load("kv1", keyvals[1].at[:, own_k], wkv.at[1, y, c], local_sem.at[4])
    load("q1", queries[1].at[own_k, :], wq.at[1, y, c], local_sem.at[5])
    load("o1", outputs[1].at[:, own_part], wo.at[1, y, x_lo, c], local_sem.at[6])
    swap_output(0)

    token_forward(0, 0, (0, 1))

    loads["docs"].wait()
    doc_row = jnp.broadcast_to(docs_in[pl.ds(inst, 1), :], (ROWS, ROWS)).astype(F32)
    place_t = lax.broadcasted_iota(jnp.int32, (ROWS, ROWS), 0)
    place_s = lax.broadcasted_iota(jnp.int32, (ROWS, ROWS), 1)
    doc_col = dot_nt((place_t == place_s).astype(BF16), doc_row.astype(BF16))
    allowed = (doc_col == doc_row) & (place_s <= place_t)
    mask[...] = jnp.zeros_like(mask)
    mask[:, :ROWS] = jnp.where(allowed, 1.0, 0.0)
    tail_pad[...] = jnp.zeros_like(tail_pad)

    lane_at = lax.broadcasted_iota(jnp.int32, (ROWS, HEAD), 1)
    select = (
        lax.broadcasted_iota(jnp.int32, (PIECE, HEAD), 0)
        == lax.broadcasted_iota(jnp.int32, (PIECE, HEAD), 1)
    ).astype(BF16)

    def pack(ref, q, tail, squares):
        high = squares.astype(BF16).astype(F32)
        low = squares - high
        tail = jnp.where(lane_at < PIECE, tail, jnp.where(lane_at == PIECE, high, 0.0))
        tail = jnp.where(lane_at == PIECE + 1, low, tail)
        ref[:, :HEAD] = q.astype(BF16)
        ref[:, HEAD:] = tail.astype(BF16)

    def squares_of(tail):
        return jnp.sum(jnp.where(lane_at < PIECE, 0.0, tail), axis=1, keepdims=True)

    def clear():
        aq[...] = jnp.zeros_like(aq)
        akv[...] = jnp.zeros_like(akv)
        ass[...] = jnp.zeros_like(ass)

    def project_one(own, first, count):
        k = x_hi if own else 1 - x_hi

        def body(j, carry):
            b = (first + j) % nz
            x = xs_own[b] if own else jnp.concatenate([xs[b, 0], xs[b, 1]], axis=1)
            xf = x.astype(F32)
            sq = xf * xf
            ass[k] += sq[:, :HEAD] + sq[:, HEAD:WIDE] + sq[:, WIDE : WIDE + HEAD] + sq[:, WIDE + HEAD :]
            aq[c, k] += jnp.dot(x, wq[0, b].reshape(2 * WIDE, HEAD), preferred_element_type=F32)
            turned = jnp.concatenate([wkv[0, b, 0], wkv[0, b, 1]], axis=1)
            akv[c, k, :, :PIECE] += dot_nt(x, turned)
            return carry

        lax.fori_loop(0, count, body, 0)

    def project(layer, first, count):
        def body(j, carry):
            b = (first + j) % nz
            x = jnp.concatenate([xs_two[b, 0].reshape(2 * ROWS, HEAD), xs_two[b, 1].reshape(2 * ROWS, HEAD)], axis=1)
            w = jnp.concatenate([wq[layer, b, 0], wq[layer, b, 1]], axis=1)
            q = jnp.dot(x, w, preferred_element_type=F32).reshape(2, ROWS, WIDE)
            xf = x.astype(F32)
            sq = (xf[:, :HEAD] * xf[:, :HEAD] + xf[:, HEAD:] * xf[:, HEAD:]).reshape(2, ROWS, HEAD)
            ass[...] += sq
            for h in range(2):
                aq[h] += q[:, :, h * HEAD : (h + 1) * HEAD]
                akv[h, :, :, :PIECE] += dot_nt(x, wkv[layer, b, h]).reshape(2, ROWS, PIECE)
            return carry

        lax.fori_loop(0, count, body, 0)

    def heads(layer, beside_step):
        for k in (1 - x_hi, x_hi) if layer == 1 else ():
            squares = jnp.sum(ass[k], axis=1, keepdims=True)
            pack(near_s.at[layer, k], aq[1 - c, k], akv[1 - c, k], squares)
            send(near_s.at[layer, k], near_r.at[layer, k], near_ss.at[layer, k], near_rs.at[layer, k], mate)
        beside_step(2)

        def chip_sum(k):
            squares = jnp.sum(ass[k], axis=1, keepdims=True)
            tail = jnp.where(lane_at < PIECE, akv[c, k], jnp.where(lane_at == PIECE, squares, 0.0))
            if layer == 0:
                return aq[c, k], tail
            landed(near_r.at[layer, k], near_ss.at[layer, k], near_rs.at[layer, k])
            other = near_r[layer, k].astype(F32)
            return aq[c, k] + other[:, :HEAD], tail + other[:, HEAD:]

        q, tail = chip_sum(1 - x_hi)
        pack(far_s.at[layer], q, tail, squares_of(tail))
        send(far_s.at[layer], far_r.at[layer], far_ss.at[layer], far_rs.at[layer], across)
        beside_step(3)
        drain(30)
        q, tail = chip_sum(x_hi)
        landed(far_r.at[layer], far_ss.at[layer], far_rs.at[layer])
        other = far_r[layer].astype(F32)
        q = q + other[:, :HEAD]
        tail = tail + other[:, HEAD:]
        scale = lax.rsqrt(squares_of(tail) * (1.0 / model) + 1e-06)
        q = (q * scale * HEAD**-0.5).astype(BF16)
        tail_pad[:ROWS, :] = jnp.where(lane_at < PIECE, tail * scale, 0.0).astype(BF16)
        kvs[layer, piece] = dot_nt(select, tail_pad[...]).astype(BF16)
        for n, peer in enumerate(sharers):
            ref = kvs.at[layer, piece]
            send(ref, ref, kv_ss.at[layer, n], kv_rs.at[layer, piece], peer)
        beside_step(4)
        for o in range(1, GROUP):
            p = (piece + o) % GROUP
            landed(kvs.at[layer, p], kv_ss.at[layer, 0], kv_rs.at[layer, p])
        keys = kvs[layer, 0:4].reshape(HEAD, WIDE)
        values = kvs[layer, 4:8].reshape(HEAD, WIDE)
        scores = jnp.dot(q, keys, preferred_element_type=F32)
        scores = jnp.where(mask[...] > 0.5, scores, -1e30)
        top = jnp.max(scores, axis=1, keepdims=True)
        weights = jnp.exp(scores - top)
        probs = (weights / jnp.sum(weights, axis=1, keepdims=True)).astype(BF16)
        place = 2 * x_lo + c
        ctx[layer, x_hi, place] = dot_nt(probs, values).astype(BF16)
        peers = (beside, beside_mate, across, mate, across_beside, across_beside_mate)
        spread(layer, x_hi, peers, 0)
        beside_step(5)

    def spread(layer, k, peers, first):
        ref = ctx.at[layer, k, 2 * x_lo + c]
        for n, peer in enumerate(peers):
            send(ref, ref, ctx_ss.at[layer, first + n], ctx_rs.at[layer, k, 2 * x_lo + c], peer)

    def spread_in(layer, k, place):
        landed(ctx.at[layer, k, place], ctx_ss.at[layer, 0], ctx_rs.at[layer, k, place])

    def reduce(layer, beside_step):
        ks = (x_hi, 1 - x_hi)
        others = (2 * x_lo + 1 - c, 2 * (1 - x_lo) + c, 2 * (1 - x_lo) + 1 - c)

        def products(k, first, last):
            left = jnp.concatenate([ctx[layer, k, n] for n in range(4)], axis=1)

            def body(j, carry):
                b, b_next = (z + 3 + 2 * j) % nz, (z + 4 + 2 * j) % nz
                right = jnp.concatenate(
                    [wo[layer, b].reshape(4 * HEAD, HEAD), wo[layer, b_next].reshape(4 * HEAD, HEAD)], axis=1
                )
                both = jnp.dot(left, right, preferred_element_type=F32)
                pbuf[b, k] = both[:, :HEAD]
                pbuf[b_next, k] = both[:, HEAD:]
                return carry

            lax.fori_loop(first, last, body, 0)

        def block(way, distance):
            return (z + (distance if way == 0 else nz - distance)) % nz

        def put(lane, way, message, value, peers):
            rs_s[layer, lane, way, message] = value.astype(BF16)
            send(
                rs_s.at[layer, lane, way, message],
                rs_r.at[layer, lane, way, message],
                z_ss.at[layer, lane, way, message],
                z_rs.at[layer, lane, way, message],
                peers[way],
            )

        def got(lane, way, message):
            landed(
                rs_r.at[layer, lane, way, message],
                z_ss.at[layer, lane, way, message],
                z_rs.at[layer, lane, way, message],
            )
            return rs_r[layer, lane, way, message].astype(F32)

        def set_out(lane):
            k = ks[lane]
            products(k, 0, 2)
            put(lane, lane, 0, pbuf[block(lane, 4), k], z_second)
            for way in range(2):
                put(lane, way, 1, pbuf[block(way, 3), k], z_next)
            products(k, 2, nz // 2)
            for way in range(2):
                put(lane, way, 3, pbuf[block(way, 1), k], z_next)

        def pass_on(lane):
            for way in range(2):
                value = pbuf[block(way, 2), ks[lane]] + got(lane, way, 1)
                if way == lane:
                    value = value + got(lane, way, 0)
                put(lane, way, 2, value, z_second)

        beside_step(1)
        for place in others:
            spread_in(layer, x_hi, place)
        output_step(layer, 5)
        set_out(0)
        spread_in(layer, 1 - x_hi, 2 * x_lo + c)
        spread(layer, 1 - x_hi, (mate,), 6)
        for place in others:
            spread_in(layer, 1 - x_hi, place)
        set_out(1)
        beside_step(2)
        pass_on(0)
        pass_on(1)
        beside_step(3)
        drain(30)

        def collected(lane):
            total = pbuf[z, ks[lane]]
            for way in range(2):
                total = total + got(lane, way, 3) + got(lane, way, 2)
            k = ks[lane]
            if layer == 0:
                if lane == 0:
                    old = xs_own[z, :, pl.ds(pl.multiple_of(c * WIDE + x_lo * HEAD, HEAD), HEAD)]
                else:
                    old = xs[z, c, :, pl.ds(pl.multiple_of(x_lo * HEAD, HEAD), HEAD)]
            else:
                old = xs_two[z, x_lo, k]
            return (old.astype(F32) + total).astype(BF16)

        return collected

    def nothing(step):
        pass

    clear()
    for b in range(nz):
        loads[("x", b)].wait()
    query_step(0, 2)
    token_forward(1, 2, (1,))
    token_forward(2, 6, (0,))
    swap_query(1)
    swap_output(1)
    query_step(0, 3)
    output_step(0, 1)
    query_ready(0)
    project_one(True, y + ny - 2, 5)
    token_close()
    query_step(0, 4)
    token_finish()
    project_one(True, y + 3, 1)
    project_one(True, y + ny - 3, 1)
    project_one(False, y + ny - 3, ny - 1)
    output_step(0, 2)
    query_step(0, 5)
    project_one(False, y + 4, 1)
    project_one(True, y + 4, 1)

    def beside_heads(step):
        if step in (3, 4):
            output_step(0, step)

    heads(0, beside_heads)
    collected = reduce(0, lambda step: query_open(1) if step == 1 else query_step(1, step))
    def gather_step(step):
        def lane_of(lane):
            k = x_hi if lane < 2 else 1 - x_hi
            half = x_lo if lane % 2 == 0 else 1 - x_lo
            reach = REACH[(lane // 2 + lane) % 2]
            return lambda b: xs_two.at[b, half, k], reach, ag_ss.at[lane], ag_rs.at[lane], lane % 2 == 0

        ring_step(step, [lane_of(lane) for lane in range(4)], z, nz, z_next)

    for lane in range(2):
        k = x_hi if lane == 0 else 1 - x_hi
        xs_two[z, x_lo, k] = collected(lane)
        ref = xs_two.at[z, x_lo, k]
        for way in range(2):
            send(ref, ref, ag_ss.at[2 * lane, way, 0], ag_rs.at[2 * lane, way, 0], z_next[way])
        for way in range(2):
            send(ref, ref, ag_ss.at[2 * lane + 1, way, 0], ag_rs.at[2 * lane + 1, way, 0], diagonal[way])
        send(ref, ref, one_ss.at[1 + lane], one_rs.at[1 + k], beside)
    clear()
    gather_step(2)
    query_step(1, 4)
    gather_step(3)
    gather_step(4)
    query_step(1, 5)
    for k in range(2):
        landed(xs_two.at[z, 1 - x_lo, k], one_ss.at[1 + k], one_rs.at[1 + k])
    query_ready(1)
    project(1, z + nz - 3, nz - 1)
    gather_step(5)
    project(1, z + 4, 1)
    heads(1, lambda step: output_step(1, step - 1))
    collected = reduce(1, nothing)
    own_half = pl.ds(pl.multiple_of(x_lo * HEAD, HEAD), HEAD)

    def deliver(lane):
        k = x_hi if lane == 0 else 1 - x_hi
        goal = ((2 * y + k + 1) % ninst, 4 * z + 2 * x_hi + c)
        return copy(fin.at[lane], out.at[:, own_half], fin_ss.at[lane], fin_rs.at[x_lo], goal)

    fin[0] = collected(0)
    deliver(0).start()
    fin[1] = collected(1)

    @pl.when(stays == 0)
    def _():
        deliver(1).start()
        deliver(1).wait_send()

    @pl.when(stays == 1)
    def _():
        keep = pltpu.make_async_copy(fin.at[1], out.at[:, own_half], local_sem.at[0])
        keep.start()
        keep.wait()

    deliver(0).wait_send()
    drain(0)
    landed(out.at[:, :HEAD], fin_ss.at[0], fin_rs.at[0])

    @pl.when(stays == 0)
    def _():
        landed(out.at[:, HEAD:], fin_ss.at[1], fin_rs.at[1])


def solution(mesh):
    ny, nz = mesh.shape["inst"] // 2, mesh.shape["tp"] // 4

    def shards(tokens, docs, q1, kv1, o1, q2, kv2, o2):
        operands = [pltpu.with_memory_space_constraint(a, pltpu.HBM) for a in (tokens, docs, q1, kv1.T, o1, q2, kv2.T, o2)]
        dma = pltpu.SemaphoreType.DMA
        anywhere = pl.BlockSpec(memory_space=pltpu.HBM)
        vmem = pltpu.VMEM
        return pl.pallas_call(
            functools.partial(kernel, ny, nz),
            out_shape=jax.ShapeDtypeStruct((ROWS, WIDE), BF16),
            in_specs=[anywhere] * 8,
            out_specs=anywhere,
            scratch_shapes=[
                vmem((2, ny, 2, WIDE, HEAD), BF16),
                vmem((2, ny, 2, PIECE, WIDE), BF16),
                vmem((2, ny, 2, 2, HEAD, HEAD), BF16),
                vmem((2 * ny, ROWS), jnp.int32),
                vmem((ROWS, WIDE), F32),
                vmem((nz, 2, ROWS, WIDE), BF16),
                vmem((nz, ROWS, 2 * WIDE), BF16),
                vmem((nz, 2, 2, ROWS, HEAD), BF16),
                vmem((2, 2, ROWS, HEAD), F32),
                vmem((2, 2, ROWS, HEAD), F32),
                vmem((2, ROWS, HEAD), F32),
                vmem((2, 2, ROWS, WIDE), BF16),
                vmem((2, 2, ROWS, WIDE), BF16),
                vmem((2, ROWS, WIDE), BF16),
                vmem((2, ROWS, WIDE), BF16),
                vmem((WIDE, HEAD), BF16),
                vmem((2, GROUP, PIECE, WIDE), BF16),
                vmem((2, 2, 4, ROWS, HEAD), BF16),
                vmem((nz, 2, ROWS, HEAD), F32),
                vmem((2, 2, 2, 4, ROWS, HEAD), BF16),
                vmem((2, 2, 2, 4, ROWS, HEAD), BF16),
                vmem((2, ROWS, HEAD), BF16),
                dma((7,)),
                dma((4,)),
                dma((nz,)),
                dma((2, 5)),
                dma((2, 5)),
                dma((20, 2, 4)),
                dma((20, 2, 4)),
                dma((4,)),
                dma((4,)),
                dma((nz,)),
                dma((nz,)),
                dma((2, 2)),
                dma((2, 2)),
                dma((2, 2)),
                dma((2, 2)),
                dma((2,)),
                dma((2,)),
                dma((2, GROUP)),
                dma((2, GROUP)),
                dma((2, 7)),
                dma((2, 2, 4)),
                dma((2, 2, 2, 4)),
                dma((2, 2, 2, 4)),
                dma((4, 2, 4)),
                dma((4, 2, 4)),
                dma((4,)),
                dma((4,)),
                dma((2,)),
                dma((2,)),
            ],
            compiler_params=pltpu.CompilerParams(
                collective_id=0,
                has_side_effects=True,
                vmem_limit_bytes=40 * 1024 * 1024,
            ),
            cost_estimate=pl.CostEstimate(
                flops=2_000_000_000, bytes_accessed=10_000_000, transcendentals=51200
            ),
        )(*operands)

    placed = (
        P("inst", None),
        P(),
        P("inst", "tp"),
        P("inst", "tp"),
        P("tp", "inst"),
        P("inst", "tp"),
        P("inst", "tp"),
        P("tp", "inst"),
    )
    return jax.shard_map(
        shards, mesh=mesh, in_specs=placed, out_specs=P("inst", "tp"), check_vma=False
    )
```

```python
import functools

import jax
import jax.numpy as jnp
from jax import lax
from jax.experimental import pallas as pl
from jax.experimental.pallas import tpu as pltpu
from jax.sharding import PartitionSpec as P

MESH = pl.DeviceIdType.MESH
F32 = jnp.float32
BF16 = jnp.bfloat16
NT = (((1,), (1,)), ((), ()))
ROWS = 160
HEAD = 128
PIECE = 32
WIDE = 256
GROUP = 8
REACH = ((4, 3), (3, 4))


def dot_nt(left, right):
    return lax.dot_general(left, right, NT, preferred_element_type=F32)


def kernel(
    ny,
    nz,
    tokens,
    docs,
    query_one,
    keyval_one,
    output_one,
    query_two,
    keyval_two,
    output_two,
    out,
    wq,
    wkv,
    wo,
    docs_in,
    mask,
    xs,
    xs_own,
    xs_two,
    aq,
    akv,
    ass,
    near_s,
    near_r,
    far_s,
    far_r,
    tail_pad,
    kvs,
    ctx,
    pbuf,
    rs_s,
    rs_r,
    fin,
    local_sem,
    own_sem,
    xlocal_sem,
    swap_ss,
    swap_rs,
    y_ss,
    y_rs,
    far_tok_ss,
    far_tok_rs,
    mate_tok_ss,
    mate_tok_rs,
    tok_ss,
    tok_rs,
    near_ss,
    near_rs,
    far_ss,
    far_rs,
    kv_ss,
    kv_rs,
    ctx_ss,
    ctx_rs,
    z_ss,
    z_rs,
    ag_ss,
    ag_rs,
    one_ss,
    one_rs,
    fin_ss,
    fin_rs,
):
    inst = lax.axis_index("inst")
    rank = lax.axis_index("tp")
    ninst, nrank = 2 * ny, 4 * nz
    y, x_hi = inst // 2, inst % 2
    z, x_lo, c = rank // 4, rank // 2 % 2, rank % 2
    piece = rank % GROUP
    model = ny * 2 * 512

    mate = (inst, rank + 1 - 2 * c)
    across = (inst + 1 - 2 * x_hi, rank)
    beside = (inst, rank + 2 - 4 * x_lo)
    y_next = (((inst + 2) % ninst, rank), ((inst + ninst - 2) % ninst, rank))
    y_next_mate = tuple((peer, rank + 1 - 2 * c) for peer, _ in y_next)
    z_next = ((inst, (rank + 4) % nrank), (inst, (rank + nrank - 4) % nrank))
    across_beside = (inst + 1 - 2 * x_hi, rank + 2 - 4 * x_lo)
    across_beside_mate = (inst + 1 - 2 * x_hi, rank + 3 - 4 * x_lo - 2 * c)
    beside_mate = (inst, rank + 3 - 4 * x_lo - 2 * c)
    origin_inst = (inst + ninst - 1) % ninst // 2 * 2 + x_lo
    origins = [(origin_inst, 4 * z + 2 * s + c) for s in range(2)]
    stays = x_hi * x_lo

    group_base = rank // GROUP * GROUP
    sharers = [(inst, group_base + (piece + o) % GROUP) for o in range(1, GROUP)]
    other_rank = (rank + nrank + 4 * (2 * (z % 2) - 1)) % nrank
    other_z = (inst, other_rank)
    other_diagonal = (inst, other_rank + 2 - 4 * x_lo)
    z_second = ((inst, (rank + 8) % nrank), (inst, (rank + nrank - 8) % nrank))
    diagonal = tuple((inst, peer + 2 - 4 * x_lo) for _, peer in z_next)

    barrier = pltpu.get_barrier_semaphore()
    greeted = [*y_next, across_beside, *y_next_mate, *sharers, other_z, other_diagonal, *z_second]
    greeted += [across, across_beside_mate, origins[0]]
    for peer in greeted:
        pl.semaphore_signal(barrier, inc=1, device_id=peer, device_id_type=MESH)

    @pl.when(stays == 0)
    def _():
        pl.semaphore_signal(barrier, inc=1, device_id=origins[1], device_id_type=MESH)

    sent = []

    def copy(src, dst, send, recv, peer):
        return pltpu.make_async_remote_copy(
            src_ref=src,
            dst_ref=dst,
            send_sem=send,
            recv_sem=recv,
            device_id=peer,
            device_id_type=MESH,
        )

    def send(*args):
        move = copy(*args)
        move.start()
        sent.append(move)

    def drain(kept):
        while len(sent) > kept:
            sent.pop(0).wait_send()

    def landed(dst, send_sem, recv_sem):
        copy(dst, dst, send_sem, recv_sem, mate).wait_recv()

    queries = (query_one, query_two)
    keyvals = (keyval_one, keyval_two)
    outputs = (output_one, output_two)
    loads = {}

    def load(name, src, dst, sem):
        loads[name] = pltpu.make_async_copy(src, dst, sem)
        loads[name].start()

    def quarter(block, hi):
        return pl.ds(pl.multiple_of((2 * block + hi) * 512 + c * WIDE, WIDE), WIDE)

    own_k = pl.ds(pl.multiple_of(c * WIDE, WIDE), WIDE)
    mate_k = pl.ds(pl.multiple_of((1 - c) * WIDE, WIDE), WIDE)
    halves = [pl.ds(half * WIDE, WIDE) for half in range(2)]
    pl.semaphore_wait(barrier, len(greeted) + 1 - stays)

    def swap(layer, n, src, dst, peer):
        send(src, dst, swap_ss.at[layer, n], swap_rs.at[layer, n], peer)

    def swapped(layer, n, dst):
        landed(dst, swap_ss.at[layer, n], swap_rs.at[layer, n])

    def swap_query(layer):
        swap(layer, 0, queries[layer].at[mate_k, :], wq.at[layer, y, c], mate)
        swap(layer, 1, keyvals[layer].at[:, mate_k], wkv.at[layer, y, c], mate)

    def part(lo, core):
        return pl.ds(pl.multiple_of((2 * core + lo) * HEAD, HEAD), HEAD)

    def swap_output(layer):
        dst = wo.at[layer, y, x_lo, c]
        swap(layer, 2, outputs[layer].at[:, part(x_lo, 1 - c)], dst, mate)
        swap(layer, 3, outputs[layer].at[:, part(1 - x_lo, c)], dst, beside)
        swap(layer, 4, outputs[layer].at[:, part(1 - x_lo, 1 - c)], dst, beside_mate)

    def ring_step(step, lanes, me, n, peers):
        for slot, reach, ss, rs, opens in lanes:
            for way in range(2):
                block = (me + (n - 1 if way == 0 else 1) * (step - 1)) % n
                if 1 < step <= reach[way] + 1:
                    landed(slot(block), ss.at[way, step - 2], rs.at[way, step - 2])
                if step <= reach[way] and (opens or step > 1):
                    ref = slot(block)
                    send(ref, ref, ss.at[way, step - 1], rs.at[way, step - 1], peers[way])

    def query_open(layer):
        for way in range(2):
            if layer == 0:
                for half in range(2):
                    for part in range(2):
                        unit = 2 * half + part
                        rows = pl.ds(half * WIDE + part * HEAD, HEAD)
                        dst = wq.at[0, y, half, pl.ds(part * HEAD, HEAD)]
                        send(queries[0].at[rows, :], dst, y_ss.at[unit, way, 0], y_rs.at[unit, way, 0], y_next[way])
                    src = keyvals[0].at[:, halves[half]]
                    unit = 4 + half
                    send(src, wkv.at[0, y, half], y_ss.at[unit, way, 0], y_rs.at[unit, way, 0], y_next[way])
                continue
            for keep in range(2):
                core = c if keep == 0 else 1 - c
                peer = y_next[way] if keep == 0 else y_next_mate[way]
                for part in range(2):
                    unit = 10 * layer + 2 * keep + part
                    rows = pl.ds(pl.multiple_of(core * WIDE + part * HEAD, HEAD), HEAD)
                    dst = wq.at[layer, y, c, pl.ds(part * HEAD, HEAD)]
                    send(queries[layer].at[rows, :], dst, y_ss.at[unit, way, 0], y_rs.at[unit, way, 0], peer)
                unit = 10 * layer + 4 + keep
                src = keyvals[layer].at[:, own_k if keep == 0 else mate_k]
                send(src, wkv.at[layer, y, c], y_ss.at[unit, way, 0], y_rs.at[unit, way, 0], peer)

    def query_step(layer, step):
        def lane_of(lane):
            keep = lane // 2 if lane < 4 else lane - 4
            head = keep if layer == 0 else c if keep == 0 else 1 - c
            rows = pl.ds(lane % 2 * HEAD, HEAD)

            def slot(b):
                return wq.at[layer, b, head, rows] if lane < 4 else wkv.at[layer, b, head]

            unit = 10 * layer + lane
            return slot, REACH[lane % 2], y_ss.at[unit], y_rs.at[unit], False

        ring_step(step, [lane_of(lane) for lane in range(6)], y, ny, y_next)

    def query_ready(layer):
        if layer == 0:
            for half in range(2):
                loads["q0", half].wait()
                loads["kv0", half].wait()
            return
        loads[f"q{layer}"].wait()
        loads[f"kv{layer}"].wait()
        swapped(layer, 0, wq.at[layer, y, 1 - c])
        swapped(layer, 1, wkv.at[layer, y, 1 - c])

    def output_step(layer, step):
        def lane_of(lane):
            lo = x_lo if lane < 2 else 1 - x_lo
            core = c if lane % 2 == 0 else 1 - c
            unit = 10 * layer + 6 + lane
            return lambda b: wo.at[layer, b, lo, core], REACH[lane % 2], y_ss.at[unit], y_rs.at[unit], True

        if step == 1:
            loads[f"o{layer}"].wait()
            for lane in range(1, 4):
                lo = x_lo if lane < 2 else 1 - x_lo
                swapped(layer, 1 + lane, wo.at[layer, y, lo, c if lane % 2 == 0 else 1 - c])
        ring_step(step, [lane_of(lane) for lane in range(4)], y, ny, y_next)

    def token_block(offset):
        return xs.at[(z + offset) % nz, c]

    def token_open():
        for n, offset in enumerate((0, 2, 6, 4)):
            b = (z + offset) % nz
            src = tokens.at[:, quarter(b, 1 - x_hi)]
            send(src, xs.at[b, c], far_tok_ss.at[n], far_tok_rs.at[n], across_beside)

    def token_forward(n, offset, ways):
        ref = token_block(offset)
        landed(ref, far_tok_ss.at[n], far_tok_rs.at[n])
        for way in ways:
            place = 0 if n == 0 else 1
            send(ref, ref, tok_ss.at[way, place], tok_rs.at[way, place], z_next[way])
        token_share(offset)

    def token_share(offset):
        ref = token_block(offset)
        send(ref, ref, mate_tok_ss.at[offset], mate_tok_rs.at[offset], mate)

    def token_close():
        token_forward(3, 4, ())
        for way, first, second in ((0, 7, 5), (1, 1, 3)):
            landed(token_block(first), tok_ss.at[way, 0], tok_rs.at[way, 0])
            token_share(first)
            landed(token_block(second), tok_ss.at[way, 1], tok_rs.at[way, 1])
            token_share(second)

    def token_finish():
        for offset in range(nz):
            landed(xs.at[(z + offset) % nz, 1 - c], mate_tok_ss.at[offset], mate_tok_rs.at[offset])

    query_open(0)
    token_open()
    own_part = pl.ds(pl.multiple_of((2 * c + x_lo) * HEAD, HEAD), HEAD)
    for half in range(2):
        load(("kv0", half), keyvals[0].at[:, halves[half]], wkv.at[0, y, half], own_sem.at[half])
        load(("q0", half), queries[0].at[halves[half], :], wq.at[0, y, half], own_sem.at[2 + half])
    for b in range(nz):
        columns = pl.ds(pl.multiple_of((2 * b + x_hi) * 512, 512), 512)
        load(("x", b), tokens.at[:, columns], xs_own.at[b], xlocal_sem.at[b])
    load("o0", outputs[0].at[:, own_part], wo.at[0, y, x_lo, c], local_sem.at[2])
    load("docs", docs, docs_in, local_sem.at[3])
    load("kv1", keyvals[1].at[:, own_k], wkv.at[1, y, c], local_sem.at[4])
    load("q1", queries[1].at[own_k, :], wq.at[1, y, c], local_sem.at[5])
    load("o1", outputs[1].at[:, own_part], wo.at[1, y, x_lo, c], local_sem.at[6])
    swap_output(0)

    token_forward(0, 0, (0, 1))

    loads["docs"].wait()
    doc_row = jnp.broadcast_to(docs_in[pl.ds(inst, 1), :], (ROWS, ROWS)).astype(F32)
    place_t = lax.broadcasted_iota(jnp.int32, (ROWS, ROWS), 0)
    place_s = lax.broadcasted_iota(jnp.int32, (ROWS, ROWS), 1)
    doc_col = dot_nt((place_t == place_s).astype(BF16), doc_row.astype(BF16))
    allowed = (doc_col == doc_row) & (place_s <= place_t)
    mask[...] = jnp.zeros_like(mask)
    mask[:, :ROWS] = jnp.where(allowed, 1.0, 0.0)
    tail_pad[...] = jnp.zeros_like(tail_pad)

    lane_at = lax.broadcasted_iota(jnp.int32, (ROWS, HEAD), 1)
    select = (
        lax.broadcasted_iota(jnp.int32, (PIECE, HEAD), 0)
        == lax.broadcasted_iota(jnp.int32, (PIECE, HEAD), 1)
    ).astype(BF16)

    def pack(ref, q, tail, squares):
        high = squares.astype(BF16).astype(F32)
        low = squares - high
        tail = jnp.where(lane_at < PIECE, tail, jnp.where(lane_at == PIECE, high, 0.0))
        tail = jnp.where(lane_at == PIECE + 1, low, tail)
        ref[:, :HEAD] = q.astype(BF16)
        ref[:, HEAD:] = tail.astype(BF16)

    def squares_of(tail):
        return jnp.sum(jnp.where(lane_at < PIECE, 0.0, tail), axis=1, keepdims=True)

    def clear():
        aq[...] = jnp.zeros_like(aq)
        akv[...] = jnp.zeros_like(akv)
        ass[...] = jnp.zeros_like(ass)

    def project_one(own, first, count):
        k = x_hi if own else 1 - x_hi

        def body(j, carry):
            b = (first + j) % nz
            x = xs_own[b] if own else jnp.concatenate([xs[b, 0], xs[b, 1]], axis=1)
            xf = x.astype(F32)
            sq = xf * xf
            ass[k] += sq[:, :HEAD] + sq[:, HEAD:WIDE] + sq[:, WIDE : WIDE + HEAD] + sq[:, WIDE + HEAD :]
            aq[c, k] += jnp.dot(x, wq[0, b].reshape(2 * WIDE, HEAD), preferred_element_type=F32)
            turned = jnp.concatenate([wkv[0, b, 0], wkv[0, b, 1]], axis=1)
            akv[c, k, :, :PIECE] += dot_nt(x, turned)
            return carry

        lax.fori_loop(0, count, body, 0)

    def project(layer, first, count):
        def body(j, carry):
            b = (first + j) % nz
            x = jnp.concatenate([xs_two[b, 0].reshape(2 * ROWS, HEAD), xs_two[b, 1].reshape(2 * ROWS, HEAD)], axis=1)
            w = jnp.concatenate([wq[layer, b, 0], wq[layer, b, 1]], axis=1)
            q = jnp.dot(x, w, preferred_element_type=F32).reshape(2, ROWS, WIDE)
            xf = x.astype(F32)
            sq = (xf[:, :HEAD] * xf[:, :HEAD] + xf[:, HEAD:] * xf[:, HEAD:]).reshape(2, ROWS, HEAD)
            ass[...] += sq
            for h in range(2):
                aq[h] += q[:, :, h * HEAD : (h + 1) * HEAD]
                akv[h, :, :, :PIECE] += dot_nt(x, wkv[layer, b, h]).reshape(2, ROWS, PIECE)
            return carry

        lax.fori_loop(0, count, body, 0)

    def heads(layer, beside_step):
        for k in (1 - x_hi, x_hi) if layer == 1 else ():
            squares = jnp.sum(ass[k], axis=1, keepdims=True)
            pack(near_s.at[layer, k], aq[1 - c, k], akv[1 - c, k], squares)
            send(near_s.at[layer, k], near_r.at[layer, k], near_ss.at[layer, k], near_rs.at[layer, k], mate)
        beside_step(2)

        def chip_sum(k):
            squares = jnp.sum(ass[k], axis=1, keepdims=True)
            tail = jnp.where(lane_at < PIECE, akv[c, k], jnp.where(lane_at == PIECE, squares, 0.0))
            if layer == 0:
                return aq[c, k], tail
            landed(near_r.at[layer, k], near_ss.at[layer, k], near_rs.at[layer, k])
            other = near_r[layer, k].astype(F32)
            return aq[c, k] + other[:, :HEAD], tail + other[:, HEAD:]

        q, tail = chip_sum(1 - x_hi)
        pack(far_s.at[layer], q, tail, squares_of(tail))
        send(far_s.at[layer], far_r.at[layer], far_ss.at[layer], far_rs.at[layer], across)
        beside_step(3)
        drain(30)
        q, tail = chip_sum(x_hi)
        landed(far_r.at[layer], far_ss.at[layer], far_rs.at[layer])
        other = far_r[layer].astype(F32)
        q = q + other[:, :HEAD]
        tail = tail + other[:, HEAD:]
        scale = lax.rsqrt(squares_of(tail) * (1.0 / model) + 1e-06)
        q = (q * scale * HEAD**-0.5).astype(BF16)
        tail_pad[:ROWS, :] = jnp.where(lane_at < PIECE, tail * scale, 0.0).astype(BF16)
        kvs[layer, piece] = dot_nt(select, tail_pad[...]).astype(BF16)
        for n, peer in enumerate(sharers[2:6] + sharers[:2] + sharers[6:]):
            ref = kvs.at[layer, piece]
            send(ref, ref, kv_ss.at[layer, n], kv_rs.at[layer, piece], peer)
        beside_step(4)
        for o in range(1, GROUP):
            p = (piece + o) % GROUP
            landed(kvs.at[layer, p], kv_ss.at[layer, 0], kv_rs.at[layer, p])
        keys = kvs[layer, 0:4].reshape(HEAD, WIDE)
        values = kvs[layer, 4:8].reshape(HEAD, WIDE)
        scores = jnp.dot(q, keys, preferred_element_type=F32)
        scores = jnp.where(mask[...] > 0.5, scores, -1e30)
        top = jnp.max(scores, axis=1, keepdims=True)
        weights = jnp.exp(scores - top)
        probs = (weights / jnp.sum(weights, axis=1, keepdims=True)).astype(BF16)
        place = 2 * x_lo + c
        ctx[layer, x_hi, place] = dot_nt(probs, values).astype(BF16)
        peers = (beside, beside_mate, across, mate, across_beside, across_beside_mate)
        spread(layer, x_hi, peers, 0)
        beside_step(5)

    def spread(layer, k, peers, first):
        ref = ctx.at[layer, k, 2 * x_lo + c]
        for n, peer in enumerate(peers):
            send(ref, ref, ctx_ss.at[layer, first + n], ctx_rs.at[layer, k, 2 * x_lo + c], peer)

    def spread_in(layer, k, place):
        landed(ctx.at[layer, k, place], ctx_ss.at[layer, 0], ctx_rs.at[layer, k, place])

    def reduce(layer, beside_step):
        ks = (x_hi, 1 - x_hi)
        others = (2 * x_lo + 1 - c, 2 * (1 - x_lo) + c, 2 * (1 - x_lo) + 1 - c)

        def products(k, first, last):
            left = jnp.concatenate([ctx[layer, k, n] for n in range(4)], axis=1)

            def body(j, carry):
                b, b_next = (z + 3 + 2 * j) % nz, (z + 4 + 2 * j) % nz
                right = jnp.concatenate(
                    [wo[layer, b].reshape(4 * HEAD, HEAD), wo[layer, b_next].reshape(4 * HEAD, HEAD)], axis=1
                )
                both = jnp.dot(left, right, preferred_element_type=F32)
                pbuf[b, k] = both[:, :HEAD]
                pbuf[b_next, k] = both[:, HEAD:]
                return carry

            lax.fori_loop(first, last, body, 0)

        def block(way, distance):
            return (z + (distance if way == 0 else nz - distance)) % nz

        def put(lane, way, message, value, peers):
            rs_s[layer, lane, way, message] = value.astype(BF16)
            send(
                rs_s.at[layer, lane, way, message],
                rs_r.at[layer, lane, way, message],
                z_ss.at[layer, lane, way, message],
                z_rs.at[layer, lane, way, message],
                peers[way],
            )

        def got(lane, way, message):
            landed(
                rs_r.at[layer, lane, way, message],
                z_ss.at[layer, lane, way, message],
                z_rs.at[layer, lane, way, message],
            )
            return rs_r[layer, lane, way, message].astype(F32)

        def set_out(lane):
            k = ks[lane]
            products(k, 0, 2)
            put(lane, lane, 0, pbuf[block(lane, 4), k], z_second)
            for way in range(2):
                put(lane, way, 1, pbuf[block(way, 3), k], z_next)
            products(k, 2, nz // 2)
            for way in range(2):
                put(lane, way, 3, pbuf[block(way, 1), k], z_next)

        def pass_on(lane):
            for way in range(2):
                value = pbuf[block(way, 2), ks[lane]] + got(lane, way, 1)
                if way == lane:
                    value = value + got(lane, way, 0)
                put(lane, way, 2, value, z_second)

        beside_step(1)
        for place in others:
            spread_in(layer, x_hi, place)
        output_step(layer, 5)
        set_out(0)
        spread_in(layer, 1 - x_hi, 2 * x_lo + c)
        spread(layer, 1 - x_hi, (mate,), 6)
        for place in others:
            spread_in(layer, 1 - x_hi, place)
        set_out(1)
        beside_step(2)
        pass_on(0)
        pass_on(1)
        beside_step(3)
        drain(30)

        def collected(lane):
            total = pbuf[z, ks[lane]]
            for way in range(2):
                total = total + got(lane, way, 3) + got(lane, way, 2)
            k = ks[lane]
            if layer == 0:
                if lane == 0:
                    old = xs_own[z, :, pl.ds(pl.multiple_of(c * WIDE + x_lo * HEAD, HEAD), HEAD)]
                else:
                    old = xs[z, c, :, pl.ds(pl.multiple_of(x_lo * HEAD, HEAD), HEAD)]
            else:
                old = xs_two[z, x_lo, k]
            return (old.astype(F32) + total).astype(BF16)

        return collected

    def nothing(step):
        pass

    clear()
    for b in range(nz):
        loads[("x", b)].wait()
    query_step(0, 2)
    token_forward(1, 2, (1,))
    token_forward(2, 6, (0,))
    swap_query(1)
    swap_output(1)
    query_step(0, 3)
    output_step(0, 1)
    query_ready(0)
    project_one(True, y + ny - 2, 5)
    token_close()
    query_step(0, 4)
    token_finish()
    project_one(True, y + 3, 1)
    project_one(True, y + ny - 3, 1)
    project_one(False, y + ny - 3, ny - 1)
    output_step(0, 2)
    query_step(0, 5)
    project_one(False, y + 4, 1)
    project_one(True, y + 4, 1)

    def beside_heads(step):
        if step in (3, 4):
            output_step(0, step)

    heads(0, beside_heads)
    collected = reduce(0, lambda step: query_open(1) if step == 1 else query_step(1, step))
    def gather_step(step):
        def lane_of(lane):
            k = x_hi if lane < 2 else 1 - x_hi
            half = x_lo if lane % 2 == 0 else 1 - x_lo
            reach = REACH[(lane // 2 + lane) % 2]
            return lambda b: xs_two.at[b, half, k], reach, ag_ss.at[lane], ag_rs.at[lane], lane % 2 == 0

        ring_step(step, [lane_of(lane) for lane in range(4)], z, nz, z_next)

    for lane in range(2):
        k = x_hi if lane == 0 else 1 - x_hi
        xs_two[z, x_lo, k] = collected(lane)
        ref = xs_two.at[z, x_lo, k]
        for way in range(2):
            send(ref, ref, ag_ss.at[2 * lane, way, 0], ag_rs.at[2 * lane, way, 0], z_next[way])
        for way in range(2):
            send(ref, ref, ag_ss.at[2 * lane + 1, way, 0], ag_rs.at[2 * lane + 1, way, 0], diagonal[way])
        send(ref, ref, one_ss.at[1 + lane], one_rs.at[1 + k], beside)
    clear()
    gather_step(2)
    query_step(1, 4)
    gather_step(3)
    gather_step(4)
    query_step(1, 5)
    for k in range(2):
        landed(xs_two.at[z, 1 - x_lo, k], one_ss.at[1 + k], one_rs.at[1 + k])
    query_ready(1)
    project(1, z + nz - 3, nz - 1)
    gather_step(5)
    project(1, z + 4, 1)
    heads(1, lambda step: output_step(1, step - 1))
    collected = reduce(1, nothing)
    own_half = pl.ds(pl.multiple_of(x_lo * HEAD, HEAD), HEAD)

    def deliver(lane):
        k = x_hi if lane == 0 else 1 - x_hi
        goal = ((2 * y + k + 1) % ninst, 4 * z + 2 * x_hi + c)
        return copy(fin.at[lane], out.at[:, own_half], fin_ss.at[lane], fin_rs.at[x_lo], goal)

    fin[0] = collected(0)
    deliver(0).start()
    fin[1] = collected(1)

    @pl.when(stays == 0)
    def _():
        deliver(1).start()
        deliver(1).wait_send()

    @pl.when(stays == 1)
    def _():
        keep = pltpu.make_async_copy(fin.at[1], out.at[:, own_half], local_sem.at[0])
        keep.start()
        keep.wait()

    deliver(0).wait_send()
    drain(0)
    landed(out.at[:, :HEAD], fin_ss.at[0], fin_rs.at[0])

    @pl.when(stays == 0)
    def _():
        landed(out.at[:, HEAD:], fin_ss.at[1], fin_rs.at[1])


def solution(mesh):
    ny, nz = mesh.shape["inst"] // 2, mesh.shape["tp"] // 4

    def shards(tokens, docs, q1, kv1, o1, q2, kv2, o2):
        operands = [pltpu.with_memory_space_constraint(a, pltpu.HBM) for a in (tokens, docs, q1, kv1.T, o1, q2, kv2.T, o2)]
        dma = pltpu.SemaphoreType.DMA
        anywhere = pl.BlockSpec(memory_space=pltpu.HBM)
        vmem = pltpu.VMEM
        return pl.pallas_call(
            functools.partial(kernel, ny, nz),
            out_shape=jax.ShapeDtypeStruct((ROWS, WIDE), BF16),
            in_specs=[anywhere] * 8,
            out_specs=anywhere,
            scratch_shapes=[
                vmem((2, ny, 2, WIDE, HEAD), BF16),
                vmem((2, ny, 2, PIECE, WIDE), BF16),
                vmem((2, ny, 2, 2, HEAD, HEAD), BF16),
                vmem((2 * ny, ROWS), jnp.int32),
                vmem((ROWS, WIDE), F32),
                vmem((nz, 2, ROWS, WIDE), BF16),
                vmem((nz, ROWS, 2 * WIDE), BF16),
                vmem((nz, 2, 2, ROWS, HEAD), BF16),
                vmem((2, 2, ROWS, HEAD), F32),
                vmem((2, 2, ROWS, HEAD), F32),
                vmem((2, ROWS, HEAD), F32),
                vmem((2, 2, ROWS, WIDE), BF16),
                vmem((2, 2, ROWS, WIDE), BF16),
                vmem((2, ROWS, WIDE), BF16),
                vmem((2, ROWS, WIDE), BF16),
                vmem((WIDE, HEAD), BF16),
                vmem((2, GROUP, PIECE, WIDE), BF16),
                vmem((2, 2, 4, ROWS, HEAD), BF16),
                vmem((nz, 2, ROWS, HEAD), F32),
                vmem((2, 2, 2, 4, ROWS, HEAD), BF16),
                vmem((2, 2, 2, 4, ROWS, HEAD), BF16),
                vmem((2, ROWS, HEAD), BF16),
                dma((7,)),
                dma((4,)),
                dma((nz,)),
                dma((2, 5)),
                dma((2, 5)),
                dma((20, 2, 4)),
                dma((20, 2, 4)),
                dma((4,)),
                dma((4,)),
                dma((nz,)),
                dma((nz,)),
                dma((2, 2)),
                dma((2, 2)),
                dma((2, 2)),
                dma((2, 2)),
                dma((2,)),
                dma((2,)),
                dma((2, GROUP)),
                dma((2, GROUP)),
                dma((2, 7)),
                dma((2, 2, 4)),
                dma((2, 2, 2, 4)),
                dma((2, 2, 2, 4)),
                dma((4, 2, 4)),
                dma((4, 2, 4)),
                dma((4,)),
                dma((4,)),
                dma((2,)),
                dma((2,)),
            ],
            compiler_params=pltpu.CompilerParams(
                collective_id=0,
                has_side_effects=True,
                vmem_limit_bytes=40 * 1024 * 1024,
            ),
            cost_estimate=pl.CostEstimate(
                flops=2_000_000_000, bytes_accessed=10_000_000, transcendentals=51200
            ),
        )(*operands)

    placed = (
        P("inst", None),
        P(),
        P("inst", "tp"),
        P("inst", "tp"),
        P("tp", "inst"),
        P("inst", "tp"),
        P("inst", "tp"),
        P("tp", "inst"),
    )
    return jax.shard_map(
        shards, mesh=mesh, in_specs=placed, out_specs=P("inst", "tp"), check_vma=False
    )
```
